32 devices in a mesh: depth: 4 (over y, x), trans: 8 (over z, core).
Axes of the slice: x: 2, y: 2, z: 4, core: 2. Of those that a mesh axis runs over, the one named last changes fastest.
Arguments:
- flight_fields: bfloat16 [4, 2, 2, 1024, 1024], P('depth', None, None, 'trans'), may hold values from -6 to 6
- top_fields: bfloat16 [2, 2, 1024, 1024], P(None, None, 'trans'), may hold values from -6 to 6
- slowness: float32 [4, 1024, 1024], P('depth', 'trans'), may hold values from 0.5 to 1.5
- ref_slowness: float32 [4], P('depth'), may hold values from 0.6 to 1
- flight_blocks: int32 [4], replicated, may hold values from 128 to 191
- top_block: int32 [1], replicated, may hold values from 0 to 255
Outputs:
- image: float32 [4, 1024, 1024], P('depth', 'trans')
- next_fields: bfloat16 [4, 2, 2, 1024, 1024], P('depth', None, None, 'trans')
The draws below stay inside these ranges and needn't reach their ends.
All inputs are finite; a program needn't handle non-finite values.
Results may differ from the reference program's by a relative error of at most 0.02.
Values may be sent and summed in bfloat16 or wider, within the bound.
No kernel may reach another device: no remote copies, remote signals or barrier semaphores. Data moves between devices by JAX's collectives and lax.ppermute only.
A program may use at most 64 MiB of HBM per device.

```python
import math
import jax
import jax.numpy as jnp

NX = 1024
NY = 1024
NFREQ = 256
NZ_DEV = 1
SLABS = 4
NZ = 4
N_DEPTH = 4


def block_law(key):
    base = jax.random.fold_in(key, 701)
    lowest = NFREQ // 2
    highest = 3 * NFREQ // 4 - 1
    values = jax.random.randint(jax.random.fold_in(base, 1), (SLABS,), lowest, highest + 1, dtype=jnp.int32)
    order = jax.random.permutation(jax.random.fold_in(base, 2), SLABS)
    values = values.at[order[0]].set(lowest)
    values = values.at[order[1]].set(highest)
    return values


def slowness_law(key):
    base = jax.random.fold_in(key, 702)
    return jax.random.uniform(base, (NZ,), jnp.float32, 0.6, 1.0)


def draw_flight_blocks(key, part):
    return block_law(key)


def draw_ref_slowness(key, part):
    return slowness_law(key)


def draw_flight_fields(key, part):
    blocks = block_law(key)
    levels = slowness_law(key)
    angular = 4.0 * (blocks.astype(jnp.float32) + 1.0) / NFREQ
    first_ref = levels[jnp.arange(SLABS, dtype=jnp.int32) * NZ_DEV]
    radius = angular * first_ref
    waves = 6
    base = jax.random.fold_in(key, 703)
    small_shape = (SLABS, 2, waves)
    theta = jax.random.uniform(jax.random.fold_in(base, 1), small_shape, jnp.float32, 0.0, 2.0 * math.pi)
    offset = jax.random.uniform(jax.random.fold_in(base, 2), small_shape, jnp.float32, -0.04, 0.04)
    start_phase = jax.random.uniform(jax.random.fold_in(base, 3), small_shape, jnp.float32, 0.0, 2.0 * math.pi)
    full_shape = (SLABS, 2, 2, NX, NY)
    amplitude = jnp.full(small_shape, 0.4, jnp.float32)
    noise = 0.5 * jax.random.truncated_normal(jax.random.fold_in(base, 5), -6.0, 6.0, full_shape, jnp.float32)
    wave_len = radius[:, None, None] + offset
    wave_x = wave_len * jnp.cos(theta)
    wave_y = wave_len * jnp.sin(theta)
    x_pos = jnp.arange(NX, dtype=jnp.float32)
    y_pos = jnp.arange(NY, dtype=jnp.float32)
    real_sum = jnp.zeros((SLABS, 2, NX, NY), jnp.float32)
    imag_sum = jnp.zeros((SLABS, 2, NX, NY), jnp.float32)
    for index in range(waves):
        phase = wave_x[:, :, index][:, :, None, None] * x_pos[None, None, :, None] + wave_y[:, :, index][:, :, None, None] * y_pos[None, None, None, :] + start_phase[:, :, index][:, :, None, None]
        weight = amplitude[:, :, index][:, :, None, None]
        real_sum = real_sum + weight * jnp.cos(phase)
        imag_sum = imag_sum + weight * jnp.sin(phase)
    cycle_part = jnp.stack([real_sum, imag_sum], axis=2)
    return (cycle_part + noise).astype(jnp.bfloat16)


def shard_levels(own_key, shape, shards, least, high):
    def one(axis_at, shards_of):
        steps = jax.random.uniform(jax.random.fold_in(jax.random.fold_in(own_key, 6), axis_at), (shards_of,), jnp.float32, least / len(shards), high / len(shards))
        return jnp.repeat(jnp.exp(steps), shape[axis_at] // shards_of).reshape((-1,) + (1,) * (len(shape) - axis_at - 1))

    level = one(*shards[0])
    for cut in shards[1:]:
        level = level * one(*cut)
    return level


def gaussian(stream_key, shape, spread, most, shards=(), kind=jnp.bfloat16):
    entries = spread * jax.random.normal(stream_key, shape, jnp.float32)
    if shards:
        entries = entries * shard_levels(stream_key, shape, shards, -0.22, 0.18)
    return jnp.clip(entries, -most, most).astype(kind)


def setup_inputs(seed: int = 0) -> dict:
    key_of = jax.random.split(jax.random.key(seed), 7)
    return {
        "flight_fields": draw_flight_fields(jax.random.fold_in(key_of[6], 71), 0),
        "top_fields": gaussian(key_of[1], (2, 2, NX, NY), 1.0, 6.0, ((2, 8),)),
        "slowness": jnp.clip(0.5 + 1.0 * jax.random.uniform(key_of[2], (NZ, NX, NY), jnp.float32) ** shard_levels(key_of[2], (NZ, NX, NY), ((0, 4), (1, 8)), -0.2, 0.2), 0.5, 1.5),
        "ref_slowness": draw_ref_slowness(jax.random.fold_in(key_of[6], 71), 0),
        "flight_blocks": draw_flight_blocks(jax.random.fold_in(key_of[6], 71), 0),
        "top_block": jax.random.randint(key_of[5], (1,), 0, NFREQ).astype(jnp.int32),
    }


omega_top = 4.0
step_length = 0.5

def make_table(length):
    positions = jnp.arange(length, dtype=jnp.int32)
    product = positions[:, None] * positions[None, :] % length
    angles = product.astype(jnp.float32) * (2.0 * math.pi / length)
    scaling = 1.0 / math.sqrt(length)
    return (jnp.concatenate([jnp.cos(angles), jnp.sin(angles)], axis=1) * scaling).astype(jnp.bfloat16)

def wavenumber(positions, length):
    signed = jnp.where(positions < length // 2, positions, positions - length)
    return signed.astype(jnp.float32) * (2.0 * math.pi / length)

def mix(product, along, half_size, orient):
    cosine_part = jax.lax.slice_in_dim(product, 0, half_size, axis=along)
    sine_part = jax.lax.slice_in_dim(product, half_size, 2 * half_size, axis=along)
    real_part = cosine_part[:, 0] + orient * sine_part[:, 1]
    imag_part = cosine_part[:, 1] - orient * sine_part[:, 0]
    return jnp.stack([real_part, imag_part], axis=1)

def rotate(values, cosines, sine_vals):
    real_part = values[:, 0] * cosines - values[:, 1] * sine_vals
    imag_part = values[:, 0] * sine_vals + values[:, 1] * cosines
    return jnp.stack([real_part, imag_part], axis=1)

def spectral(angular, reference_s, wave_x, wave_y):
    quad = (angular * reference_s) ** 2 - wave_x * wave_x - wave_y * wave_y
    travel = jnp.sqrt(jnp.maximum(quad, 0.0)) * step_length
    damping = jnp.exp(-jnp.sqrt(jnp.maximum(-quad, 0.0)) * step_length)
    cosines = damping * jnp.cos(travel)
    sine_vals = damping * jnp.sin(travel)
    return (jnp.stack([cosines, cosines]), jnp.stack([sine_vals, -sine_vals]))

def advance_plane(fields, angular, reference_s, slab_slow, table_x, table_y):
    float_x = table_x.astype(jnp.float32)
    float_y = table_y.astype(jnp.float32)
    product = jnp.einsum('fcxy,yk->fcxk', fields.astype(jnp.float32), float_y)
    first = mix(product, 3, NY, 1.0).astype(jnp.bfloat16)
    product = jnp.einsum('fcxk,xm->fcmk', first.astype(jnp.float32), float_x)
    spectrum = mix(product, 2, NX, 1.0)
    wave_x = wavenumber(jnp.arange(NX, dtype=jnp.int32), NX)[:, None]
    wave_y = wavenumber(jnp.arange(NY, dtype=jnp.int32), NY)[None, :]
    cosines, sine_vals = spectral(angular, reference_s, wave_x, wave_y)
    shifted = rotate(spectrum, cosines, sine_vals).astype(jnp.bfloat16)
    product = jnp.einsum('fcmk,mx->fcxk', shifted.astype(jnp.float32), float_x)
    back_x = mix(product, 2, NX, -1.0).astype(jnp.bfloat16)
    product = jnp.einsum('fcxk,ky->fcxy', back_x.astype(jnp.float32), float_y)
    space = mix(product, 3, NY, -1.0)
    rotation = angular * (slab_slow - reference_s) * step_length
    cos_r = jnp.cos(rotation)
    sin_r = jnp.sin(rotation)
    stepped = rotate(space, jnp.stack([cos_r, cos_r]), jnp.stack([sin_r, -sin_r])).astype(jnp.bfloat16)
    values = stepped.astype(jnp.float32)
    level_term = values[0, 0] * values[1, 0] + values[0, 1] * values[1, 1]
    return (stepped, level_term)

def reference(flight_fields, top_fields, slowness, ref_slowness, flight_blocks, top_block):
    table_x = make_table(NX)
    table_y = make_table(NY)

    def advance(fields, block_id, slab):
        angular = omega_top * (block_id.astype(jnp.float32) + 1.0) / NFREQ
        terms = []
        for level_idx in range(NZ_DEV):
            depth_level = slab * NZ_DEV + level_idx
            fields, level_term = advance_plane(fields, angular, ref_slowness[depth_level], slowness[depth_level], table_x, table_y)
            terms.append(level_term)
        return (fields, jnp.stack(terms))
    after_first = []
    first_terms = []
    for slab in range(N_DEPTH):
        stepped, terms = advance(flight_fields[slab], flight_blocks[slab], slab)
        after_first.append(stepped)
        first_terms.append(terms)
    second = []
    images = []
    for slab in range(N_DEPTH):
        if slab == 0:
            incoming = top_fields
            block_id = top_block[0]
        else:
            incoming = after_first[slab - 1]
            block_id = flight_blocks[slab - 1]
        stepped, terms = advance(incoming, block_id, slab)
        second.append(stepped)
        images.append(first_terms[slab] + terms)
    return (jnp.concatenate(images, axis=0), jnp.stack(second))
```

```python
import functools
import math

import jax
import jax.numpy as jnp
import numpy as np
from jax import lax
from jax.experimental import pallas as pl
from jax.experimental.pallas import tpu as pltpu
from jax.sharding import PartitionSpec as P

NFREQ = 256

omega_top = 4.0
step_length = 0.5

VMEM = pl.BlockSpec(memory_space=pltpu.VMEM)
SMEM = pl.BlockSpec(memory_space=pltpu.SMEM)
F32 = jnp.float32
BF16 = jnp.bfloat16


def cas_table(length):
    positions = np.arange(length, dtype=np.int64)
    angles = (positions[:, None] * positions[None, :] % length) * (2.0 * math.pi / length)
    return jnp.asarray((np.cos(angles) + np.sin(angles)) / math.sqrt(length), dtype=BF16)


def signed_wave(index, length):
    signed = jnp.where(index < length // 2, index, index - length)
    return signed.astype(F32) * (2.0 * math.pi / length)


def cos_sin(angle):
    square = angle * angle
    cosine = jnp.full_like(square, 1.0 / math.factorial(16))
    for order in range(14, -1, -2):
        cosine = cosine * -square + 1.0 / math.factorial(order)
    sine = jnp.full_like(square, 1.0 / math.factorial(15))
    for order in range(13, 0, -2):
        sine = sine * -square + 1.0 / math.factorial(order)
    return cosine, sine * angle


def spectral_kernel(index_ref, scalar_ref, cos_ref, sin_ref):
    length_x, modes = cos_ref.shape
    angular, reference_s = scalar_ref[0], scalar_ref[1]
    first_mode = index_ref[0] * modes
    step = 64
    length_y = index_ref[1]
    mode = first_mode + lax.broadcasted_iota(jnp.int32, (step, modes), 1)
    signed = jnp.where(mode < length_y // 2, mode, mode - length_y)
    wave_y = signed.astype(F32) * scalar_ref[2]
    constant = (angular * reference_s) ** 2 - wave_y * wave_y

    @pl.loop(0, length_x // step)
    def _(chunk):
        rows = pl.ds(pl.multiple_of(chunk * step, step), step)
        kx = chunk * step + lax.broadcasted_iota(jnp.int32, (step, modes), 0)
        wave_x = signed_wave(kx, length_x)
        quad = constant - wave_x * wave_x
        root = jnp.sqrt(jnp.abs(quad)) * step_length
        travels = quad > 0.0
        cosine, sine = cos_sin(jnp.where(travels, root, 0.0))
        damping = jnp.exp(jnp.where(travels, 0.0, -root))
        cos_ref[rows, :] = damping * cosine
        sin_ref[rows, :] = damping * sine


def phase_kernel(scalar_ref, slowness_ref, cos_ref, sin_ref):
    angular, reference_s = scalar_ref[0], scalar_ref[1]
    step = 8

    @pl.loop(0, cos_ref.shape[0] // step)
    def _(chunk):
        rows = pl.ds(pl.multiple_of(chunk * step, step), step)
        cosine, sine = cos_sin(angular * (slowness_ref[rows, :] - reference_s) * step_length)
        cos_ref[rows, :] = cosine
        sin_ref[rows, :] = sine


def split_modes(trans, whole, outs):
    rows, width = outs[0].shape
    block = width // 4
    for j, out in enumerate(outs):
        columns = pl.ds(pl.multiple_of((trans ^ j) * block, block), block)
        for part in range(4):
            out[:, part * block : (part + 1) * block] = whole[
                part * rows : (part + 1) * rows, columns
            ]


def join_modes(trans, pieces, whole):
    rows, width = pieces[0].shape
    block = width // 4
    for j, piece in enumerate(pieces):
        columns = pl.ds(pl.multiple_of((trans ^ j) * block, block), block)
        for part in range(4):
            whole[part * rows : (part + 1) * rows, columns] = piece[
                :, part * block : (part + 1) * block
            ]


def times_table(left_ref, table_ref, out_ref, step=256):
    for start in range(0, table_ref.shape[1], step):
        product = jnp.dot(
            left_ref[...], table_ref[:, start : start + step], preferred_element_type=F32
        )
        out_ref[:, start : start + step] = product.astype(BF16)


def to_modes_kernel(count, index_ref, fields_ref, table_ref, *refs):
    outs, modes = refs[:count], refs[count]
    times_table(fields_ref, table_ref, modes)
    split_modes(index_ref[0], modes, outs)


def along_x_kernel(count, index_ref, cos_ref, sin_ref, table_ref, *refs):
    pieces, outs = refs[:count], refs[count : 2 * count]
    held, shifted = refs[2 * count :]
    trans = index_ref[0]
    rows, width = outs[0].shape
    block = width // 4
    for j, piece in enumerate(pieces):
        held[pl.ds(pl.multiple_of((trans ^ j) * rows, rows), rows), :] = piece[...]
    for field in range(2):
        lanes = slice(2 * field * block, 2 * (field + 1) * block)
        spectrum = jnp.dot(table_ref[...], held[:, lanes], preferred_element_type=F32)
        real, imag = spectrum[:, :block], spectrum[:, block:]
        cosine = cos_ref[...]
        sine = sin_ref[...] if field == 0 else -sin_ref[...]
        base = 2 * field * block
        shifted[:, base : base + block] = (real * cosine - imag * sine).astype(BF16)
        shifted[:, base + block : base + 2 * block] = (real * sine + imag * cosine).astype(BF16)
    for field in range(2):
        lanes = slice(2 * field * block, 2 * (field + 1) * block)
        held[:, lanes] = jnp.dot(
            table_ref[...], shifted[:, lanes], preferred_element_type=F32
        ).astype(BF16)
    for j, out in enumerate(outs):
        out[...] = held[pl.ds(pl.multiple_of((trans ^ j) * rows, rows), rows), :]


def to_space(modes, table_ref, cos_ref, sin_ref, start, step):
    rows = cos_ref.shape[0]
    columns = slice(start, start + step)
    space = jnp.dot(modes[...], table_ref[:, columns], preferred_element_type=F32)
    cosine, sine = cos_ref[:, columns], sin_ref[:, columns]
    parts = []
    for field in range(2):
        real = space[2 * field * rows : (2 * field + 1) * rows]
        imag = space[(2 * field + 1) * rows : (2 * field + 2) * rows]
        turn = sine if field == 0 else -sine
        parts.append((real * cosine - imag * turn).astype(BF16))
        parts.append((real * turn + imag * cosine).astype(BF16))
    wide = [part.astype(F32) for part in parts]
    return parts, wide[0] * wide[2] + wide[1] * wide[3]


def turn_around_kernel(
    count, index_ref, cos_ref, sin_ref, top_ref, table_ref, *refs, step=256
):
    pieces, outs = refs[:count], refs[count : 2 * count]
    term_ref, modes, space = refs[2 * count :]
    trans = index_ref[0]
    last = index_ref[1] == 1
    rows = cos_ref.shape[0]
    join_modes(trans, pieces, modes)
    for start in range(0, table_ref.shape[1], step):
        parts, term = to_space(modes, table_ref, cos_ref, sin_ref, start, step)
        columns = slice(start, start + step)
        term_ref[:, columns] = term
        for index, part in enumerate(parts):
            lines = slice(index * rows, (index + 1) * rows)
            space[lines, columns] = jnp.where(last, top_ref[lines, columns], part)
    times_table(space, table_ref, modes, step)
    split_modes(trans, modes, outs)


def finish_kernel(
    count, index_ref, cos_ref, sin_ref, term_ref, table_ref, *refs, step=256
):
    pieces = refs[:count]
    fields_ref, image_ref, modes = refs[count:]
    rows = cos_ref.shape[0]
    join_modes(index_ref[0], pieces, modes)
    for start in range(0, table_ref.shape[1], step):
        parts, term = to_space(modes, table_ref, cos_ref, sin_ref, start, step)
        columns = slice(start, start + step)
        image_ref[:, columns] = term_ref[:, columns] + term
        for index, part in enumerate(parts):
            fields_ref[index * rows : (index + 1) * rows, columns] = part


def call(kernel, operands, specs, outs, scratch=(), flops=0, name=None):
    moved = sum(math.prod(a.shape) * a.dtype.itemsize for a in operands)
    moved += sum(math.prod(a.shape) * a.dtype.itemsize for a in outs)
    return pl.pallas_call(
        kernel,
        out_shape=tuple(outs),
        in_specs=specs,
        out_specs=tuple(VMEM for _ in outs),
        scratch_shapes=list(scratch),
        compiler_params=pltpu.CompilerParams(vmem_limit_bytes=24 * 1024 * 1024),
        cost_estimate=pl.CostEstimate(flops=flops, bytes_accessed=moved, transcendentals=0),
        name=name,
    )(*operands)


def per_device(flight_fields, top_fields, slowness, ref_slowness, flight_blocks, top_block):
    depth_count, trans_count = lax.axis_size("depth"), lax.axis_size("trans")
    rows, length_y = flight_fields.shape[3:]
    length_x = rows * trans_count
    block = length_y // trans_count
    table_x, table_y = cas_table(length_x), cas_table(length_y)
    depth, trans = lax.axis_index("depth"), lax.axis_index("trans")
    index = jnp.stack([trans, (depth == depth_count - 1).astype(jnp.int32)]).astype(jnp.int32)
    place = jnp.stack([trans, jnp.int32(length_y)]).astype(jnp.int32)
    first_block = flight_blocks[depth]
    above_block = flight_blocks[jnp.maximum(depth - 1, 0)]
    second_block = jnp.where(depth == 0, top_block[0], above_block)
    scalars = [
        jnp.stack([
            omega_top * (block_id.astype(F32) + 1.0) / NFREQ,
            ref_slowness[0],
            jnp.float32(2.0 * math.pi / length_y),
        ])
        for block_id in (first_block, second_block)
    ]
    spectra, phases = [], []
    for scalar in scalars:
        shape = jax.ShapeDtypeStruct((length_x, block), F32)
        spectra.append(
            call(spectral_kernel, (place, scalar), [SMEM, SMEM], [shape] * 2,
                 flops=100 * length_x * block, name="spectral_factors")
        )
        shape = jax.ShapeDtypeStruct((rows, length_y), F32)
        phases.append(
            call(phase_kernel, (scalar, slowness[0]), [SMEM, VMEM], [shape] * 2,
                 flops=100 * rows * length_y, name="phase_factors")
        )

    pieces_shape = [jax.ShapeDtypeStruct((rows, 4 * block), BF16)] * trans_count
    modes_scratch = pltpu.VMEM((4 * rows, length_y), BF16)
    x_scratch = pltpu.VMEM((length_x, 4 * block), BF16)
    one = 2 * 4 * rows * length_y * length_y
    two = 4 * 4 * block * length_x * length_x

    def exchange(pieces, shift=0):
        got = []
        for j, piece in enumerate(pieces):
            if shift == 0:
                pairs = [(t, t ^ j) for t in range(trans_count)]
                got.append(lax.ppermute(piece, "trans", pairs) if j else piece)
            else:
                pairs = [
                    (d * trans_count + t, (d + shift) % depth_count * trans_count + (t ^ j))
                    for d in range(depth_count)
                    for t in range(trans_count)
                ]
                got.append(lax.ppermute(piece, ("depth", "trans"), pairs))
        return got

    def along_x(pieces, factors):
        return call(
            functools.partial(along_x_kernel, trans_count),
            (index, *factors, table_x, *pieces),
            [SMEM] + [VMEM] * (3 + trans_count),
            pieces_shape, [x_scratch, x_scratch], two, "along_x",
        )

    flat = (4 * rows, length_y)
    first = call(
        functools.partial(to_modes_kernel, trans_count),
        (index, flight_fields.reshape(flat), table_y),
        [SMEM, VMEM, VMEM], pieces_shape, [modes_scratch], one, "to_modes",
    )
    back = exchange(along_x(exchange(first), spectra[0]))
    *second, terms = call(
        functools.partial(turn_around_kernel, trans_count),
        (index, *phases[0], top_fields.reshape(flat), table_y, *back),
        [SMEM] + [VMEM] * (4 + trans_count),
        pieces_shape + [jax.ShapeDtypeStruct((rows, length_y), F32)],
        [modes_scratch, modes_scratch], 2 * one, "turn_around",
    )
    back = exchange(along_x(exchange(second, 1), spectra[1]))
    fields, image = call(
        functools.partial(finish_kernel, trans_count),
        (index, *phases[1], terms, table_y, *back),
        [SMEM] + [VMEM] * (4 + trans_count),
        [jax.ShapeDtypeStruct(flat, BF16), jax.ShapeDtypeStruct((rows, length_y), F32)],
        [modes_scratch], one, "finish",
    )
    return image[None], fields.reshape(flight_fields.shape)


def passed_along(value, axis, steps):
    count = lax.axis_size(axis)
    leading, last = (max(0, -steps), min(count, count - steps))
    return lax.ppermute(value, axis, [(source, source + steps) for source in range(leading, last)])


def make_table(length):
    positions = jnp.arange(length, dtype=jnp.int32)
    product = positions[:, None] * positions[None, :] % length
    angles = product.astype(jnp.float32) * (2.0 * math.pi / length)
    scaling = 1.0 / math.sqrt(length)
    return (jnp.concatenate([jnp.cos(angles), jnp.sin(angles)], axis=1) * scaling).astype(
        jnp.bfloat16
    )


def wavenumber(positions, length):
    signed = jnp.where(positions < length // 2, positions, positions - length)
    return signed.astype(jnp.float32) * (2.0 * math.pi / length)


def mix(product, along, half_size, orient):
    cosine_part = lax.slice_in_dim(product, 0, half_size, axis=along)
    sine_part = lax.slice_in_dim(product, half_size, 2 * half_size, axis=along)
    real_part = cosine_part[:, 0] + orient * sine_part[:, 1]
    imag_part = cosine_part[:, 1] - orient * sine_part[:, 0]
    return jnp.stack([real_part, imag_part], axis=1)


def rotate(values, cosines, sine_vals):
    real_part = values[:, 0] * cosines - values[:, 1] * sine_vals
    imag_part = values[:, 0] * sine_vals + values[:, 1] * cosines
    return jnp.stack([real_part, imag_part], axis=1)


def spectral(angular, reference_s, wave_x, wave_y):
    quad = (angular * reference_s) ** 2 - wave_x * wave_x - wave_y * wave_y
    travel = jnp.sqrt(jnp.maximum(quad, 0.0)) * step_length
    damping = jnp.exp(-jnp.sqrt(jnp.maximum(-quad, 0.0)) * step_length)
    cosines = damping * jnp.cos(travel)
    sine_vals = damping * jnp.sin(travel)
    return (jnp.stack([cosines, cosines]), jnp.stack([sine_vals, -sine_vals]))


def propagate(fields, spec_cos, spec_sin, space_cos, space_sin, to_cols, to_rows, table_x, table_y):
    length_y = table_y.shape[0]
    length_x = table_x.shape[0]
    product = jnp.einsum("fcry,yk->fckr", fields, table_y, preferred_element_type=jnp.float32)
    first = mix(product, 2, length_y, 1.0).astype(jnp.bfloat16)
    columns = to_cols(first)
    product = jnp.dot(columns, table_x, preferred_element_type=jnp.float32)
    spectrum = mix(product, 3, length_x, 1.0)
    shifted = rotate(spectrum, spec_cos, spec_sin).astype(jnp.bfloat16)
    product = jnp.dot(shifted, table_x, preferred_element_type=jnp.float32)
    back_x = mix(product, 3, length_x, -1.0).astype(jnp.bfloat16)
    rows_back = to_rows(back_x)
    product = jnp.einsum("fckr,ky->fcry", rows_back, table_y, preferred_element_type=jnp.float32)
    space = mix(product, 3, length_y, -1.0)
    return rotate(space, space_cos, space_sin).astype(jnp.bfloat16)


def together_cols(values):
    return lax.all_to_all(values, "trans", split_axis=2, concat_axis=3, tiled=True)


def together_rows(values):
    return lax.all_to_all(values, "trans", split_axis=3, concat_axis=2, tiled=True)


def advance(fields, block_id, slowness, ref_slowness, table_x, table_y):
    length_x = table_x.shape[0]
    length_y = table_y.shape[0]
    trans_count = lax.axis_size("trans")
    local_ky = length_y // trans_count
    ky_rows = lax.axis_index("trans") * local_ky + jnp.arange(local_ky, dtype=jnp.int32)
    wave_y = wavenumber(ky_rows, length_y)[:, None]
    wave_x = wavenumber(jnp.arange(length_x, dtype=jnp.int32), length_x)[None, :]
    angular = omega_top * (block_id.astype(jnp.float32) + 1.0) / NFREQ
    reference_s = ref_slowness[0]
    spec_cos, spec_sin = spectral(angular, reference_s, wave_x, wave_y)
    rotation = angular * (slowness[0] - reference_s) * step_length
    cos_r = jnp.cos(rotation)
    sin_r = jnp.sin(rotation)
    space_cos = jnp.stack([cos_r, cos_r])
    space_sin = jnp.stack([sin_r, -sin_r])
    fields = propagate(
        fields,
        spec_cos,
        spec_sin,
        space_cos,
        space_sin,
        together_cols,
        together_rows,
        table_x,
        table_y,
    )
    values = fields.astype(jnp.float32)
    terms = [values[0, 0] * values[1, 0] + values[0, 1] * values[1, 1]]
    return (fields, jnp.stack(terms))


def general_per_device(flight_fields, top_fields, slowness, ref_slowness, flight_blocks, top_block):
    table_x = make_table(flight_fields.shape[3] * lax.axis_size("trans"))
    table_y = make_table(flight_fields.shape[4])
    depth_idx = lax.axis_index("depth")
    first_block = flight_blocks[depth_idx]
    above_block = flight_blocks[jnp.maximum(depth_idx - 1, 0)]
    second_block = jnp.where(depth_idx == 0, top_block[0], above_block)
    after_first, first_terms = advance(
        flight_fields[0], first_block, slowness, ref_slowness, table_x, table_y
    )
    handed = passed_along(after_first, "depth", 1)
    incoming = jnp.where(depth_idx == 0, top_fields, handed)
    after_second, second_terms = advance(
        incoming, second_block, slowness, ref_slowness, table_x, table_y
    )
    return (first_terms + second_terms, after_second[None])


def solution(mesh):
    placed = (
        P("depth", None, None, "trans", None),
        P(None, None, "trans", None),
        P("depth", "trans", None),
        P("depth"),
        P(),
        P(),
    )

    def chosen(*arrays):
        trans_count = lax.axis_size("trans")
        rows, length_y = arrays[0].shape[3:]
        whole_blocks = length_y % (128 * trans_count) == 0 and rows % 16 == 0
        paired = trans_count & (trans_count - 1) == 0
        return (per_device if whole_blocks and paired else general_per_device)(*arrays)

    return jax.shard_map(
        chosen,
        mesh=mesh,
        in_specs=placed,
        out_specs=(P("depth", "trans", None), P("depth", None, None, "trans", None)),
        check_vma=False,
    )
```

```python
import functools
import math

import jax
import jax.numpy as jnp
import numpy as np
from jax import lax
from jax.experimental import pallas as pl
from jax.experimental.pallas import tpu as pltpu
from jax.sharding import Mesh, PartitionSpec as P

NFREQ = 256

omega_top = 4.0
step_length = 0.5

VMEM = pl.BlockSpec(memory_space=pltpu.VMEM)
SMEM = pl.BlockSpec(memory_space=pltpu.SMEM)
F32 = jnp.float32
BF16 = jnp.bfloat16


def partners(count):
    return sorted(range(count), key=lambda k: (-k.bit_length(), k))


def cas_tables(length):
    positions = np.arange(length // 2, dtype=np.int64)

    def table(modes):
        angles = (modes[:, None] * positions[None, :] % length) * (2.0 * math.pi / length)
        return ((np.cos(angles) + np.sin(angles)) / math.sqrt(length)).astype(jnp.bfloat16)

    even, odd = table(2 * positions), table(2 * positions + 1)
    return jnp.asarray(even), jnp.asarray(odd), jnp.asarray(odd.T.copy())


def dot(left, right):
    return jnp.dot(left, right, preferred_element_type=F32)


def signed_wave(index, length):
    signed = jnp.where(index < length // 2, index, index - length)
    return signed.astype(F32) * (2.0 * math.pi / length)


def cos_sin(angle):
    square = angle * angle
    cosine = jnp.full_like(square, 1.0 / math.factorial(16))
    for order in range(14, -1, -2):
        cosine = cosine * -square + 1.0 / math.factorial(order)
    sine = jnp.full_like(square, 1.0 / math.factorial(15))
    for order in range(13, 0, -2):
        sine = sine * -square + 1.0 / math.factorial(order)
    return cosine, sine * angle


def factors_kernel(odd, length_y, place_ref, scalar_ref, cos_ref, sin_ref):
    length_x, modes = cos_ref.shape
    half = length_x // 2
    angular, reference_s, sign = scalar_ref[0], scalar_ref[1], scalar_ref[2]
    step = 64
    lane = lax.broadcasted_iota(jnp.int32, (step, modes), 1)
    line = lax.broadcasted_iota(jnp.int32, (step, modes), 0)
    wave_y = signed_wave(2 * (place_ref[0] * modes + lane) + odd, length_y)
    constant = (angular * reference_s) ** 2 - wave_y * wave_y

    @pl.loop(0, length_x // step)
    def _(chunk):
        rows = pl.ds(pl.multiple_of(chunk * step, step), step)
        place = chunk * step + line
        kx = jnp.where(place < half, 2 * place, 2 * place - length_x + 1)
        wave_x = signed_wave(kx, length_x)
        quad = constant - wave_x * wave_x
        root = jnp.sqrt(jnp.abs(quad)) * step_length
        travels = quad > 0.0
        cosine, sine = cos_sin(jnp.where(travels, root, 0.0))
        damping = jnp.exp(jnp.where(travels, 0.0, -root))
        cos_ref[rows, :] = damping * cosine
        sin_ref[rows, :] = (sign * damping) * sine


def phase_kernel(place_ref, scalar_ref, mine_ref, other_ref, cos_ref, sin_ref):
    angular, reference_s, sign = scalar_ref[0], scalar_ref[1], scalar_ref[2]
    rows = mine_ref.shape[0]
    step = 8
    for index, slowness in enumerate((mine_ref, other_ref)):
        start = (place_ref[1] ^ index) * rows

        @pl.loop(0, rows // step)
        def _(chunk):
            there = pl.ds(pl.multiple_of(start + chunk * step, step), step)
            here = pl.ds(pl.multiple_of(chunk * step, step), step)
            cosine, sine = cos_sin(angular * (slowness[here, :] - reference_s) * step_length)
            cos_ref[there, :] = cosine
            sin_ref[there, :] = sign * sine


def rows_of(start, size):
    return pl.ds(pl.multiple_of(start, size), size)


def split_modes(here, whole, outs):
    rows, width = outs[0].shape
    block = width // 2
    for k, out in zip(partners(len(outs)), outs):
        columns = rows_of((here ^ k) * block, block)
        for part in range(2):
            out[:, part * block : (part + 1) * block] = whole[
                part * rows : (part + 1) * rows, columns
            ]


def join_modes(here, pieces, whole, lines=None):
    rows, width = pieces[0].shape
    block = width // 2
    size = rows if lines is None else lines.size
    for k, piece in zip(partners(len(pieces)), pieces):
        columns = rows_of((here ^ k) * block, block)
        for part in range(2):
            whole[part * size : (part + 1) * size, columns] = piece[
                slice(None) if lines is None else lines, part * block : (part + 1) * block
            ]


def to_modes_kernel(odd, place_ref, fields_ref, other_ref, table_ref, *refs):
    outs, (folded, modes) = refs[:-2], refs[-2:]
    rows = other_ref.shape[0] // 2
    half = table_ref.shape[0]
    core = place_ref[1]
    for part in range(2):
        mine = rows_of((2 * core + part) * rows, rows)
        for lines, source, index in ((mine, fields_ref, 0), (slice(part * rows, (part + 1) * rows), other_ref, 1)):
            low, high = source[lines, :half], source[lines, half:]
            there = rows_of(2 * part * rows + (core ^ index) * rows, rows)
            folded[there, :] = low - high if odd else low + high
    modes[...] = dot(folded[...], table_ref[...]).astype(BF16)
    split_modes(place_ref[0], modes, outs)


def along_x_kernel(count, place_ref, cos_ref, sin_ref, even_ref, odd_ref, turned_ref, *refs):
    pieces, outs = refs[:count], refs[count : 2 * count]
    held, shifted = refs[2 * count :]
    here = place_ref[0]
    rows, width = outs[0].shape
    block = width // 2
    for k, piece in zip(partners(count), pieces):
        held[rows_of((here ^ k) * rows, rows), :] = piece[...]
    half = even_ref.shape[0]
    low, high = held[:half, :], held[half:, :]
    for part, table, values in ((0, even_ref, low + high), (1, odd_ref, low - high)):
        lines = slice(part * half, (part + 1) * half)
        spectrum = dot(table[...], values)
        real, imag = spectrum[:, :block], spectrum[:, block:]
        cosine, sine = cos_ref[lines, :], sin_ref[lines, :]
        shifted[lines, :block] = (real * cosine - imag * sine).astype(BF16)
        shifted[lines, block:] = (real * sine + imag * cosine).astype(BF16)
    first = dot(even_ref[...], shifted[:half, :])
    second = dot(turned_ref[...], shifted[half:, :])
    held[:half, :] = (first + second).astype(BF16)
    held[half:, :] = (first - second).astype(BF16)
    for k, out in zip(partners(count), outs):
        out[...] = held[rows_of((here ^ k) * rows, rows), :]


def even_part_kernel(place_ref, table_ref, *refs):
    pieces, (out_ref, modes) = refs[:-2], refs[-2:]
    join_modes(place_ref[0], pieces, modes)
    out_ref[...] = dot(modes[...], table_ref[...])


def turned(real, imag, cosine, sine):
    return (real * cosine - imag * sine).astype(BF16), (real * sine + imag * cosine).astype(BF16)


def turn_around_kernel(
    count, place_ref, cos_ref, sin_ref, top_ref, top_other_ref, even_ref, odd_ref, part_ref, *refs
):
    pieces, outs = refs[:count], refs[count : 2 * count]
    folded_ref, keep_ref, give_ref, modes, space, sums = refs[2 * count :]
    here, core = place_ref[0], place_ref[1]
    rows = pieces[0].shape[0]
    own = rows // 2
    half = odd_ref.shape[0]
    join_modes(here, pieces, modes)
    step = 256
    for start in range(0, half, step):
        columns = slice(start, start + step)
        second = dot(modes[...], odd_ref[:, columns])
        first = part_ref[:, columns]
        for values, at in ((first + second, start), (first - second, start + half)):
            lanes = slice(at, at + step)
            real, imag = turned(values[:rows], values[rows:], cos_ref[:, lanes], sin_ref[:, lanes])
            space[:rows, lanes] = real
            space[rows:, lanes] = imag
    for index, out in enumerate((keep_ref, give_ref)):
        for part in range(2):
            out[part * own : (part + 1) * own, :] = space[
                rows_of(part * rows + (core ^ index) * own, own), :
            ]

    @pl.when(place_ref[2] == 1)
    def _():
        for part in range(2):
            space[rows_of(part * rows + core * own, own), :] = top_ref[
                rows_of((2 * core + part) * own, own), :
            ]
            space[rows_of(part * rows + (core ^ 1) * own, own), :] = top_other_ref[
                part * own : (part + 1) * own, :
            ]

    sums[...] = space[:, :half] + space[:, half:]
    folded_ref[...] = space[:, :half] - space[:, half:]
    modes[...] = dot(sums[...], even_ref[...]).astype(BF16)
    split_modes(here, modes, outs)


def odd_modes_kernel(place_ref, folded_ref, table_ref, *refs):
    outs, modes = refs[:-1], refs[-1]
    modes[...] = dot(folded_ref[...], table_ref[...]).astype(BF16)
    split_modes(place_ref[0], modes, outs)


def half_space_kernel(index, place_ref, cos_ref, sin_ref, odd_ref, part_ref, *refs):
    pieces, (out_ref, modes) = refs[:-2], refs[-2:]
    rows = pieces[0].shape[0]
    own = rows // 2
    half = odd_ref.shape[0]
    offset = (place_ref[1] ^ index) * own
    lines = rows_of(offset, own)
    join_modes(place_ref[0], pieces, modes, lines)
    step = 256
    for start in range(0, half, step):
        columns = slice(start, start + step)
        second = dot(modes[...], odd_ref[:, columns])
        for sign, at in ((1.0, start), (-1.0, start + half)):
            lanes = slice(at, at + step)
            real, imag = [
                part_ref[rows_of(part * rows + offset, own), columns]
                + sign * second[part * own : (part + 1) * own]
                for part in range(2)
            ]
            out_ref[:own, lanes], out_ref[own:, lanes] = turned(
                real, imag, cos_ref[lines, lanes], sin_ref[lines, lanes]
            )


def finish_kernel(place_ref, first_ref, first_other_ref, keep_ref, got_ref, fields_ref, image_ref):
    rows = keep_ref.shape[0]
    own = rows // 2
    core = place_ref[1]
    fields_ref[rows_of(core * rows, rows), :] = keep_ref[...]
    fields_ref[rows_of((core ^ 1) * rows, rows), :] = got_ref[...]
    step = 16
    for start in range(0, own, step):
        total = None
        for one, two in ((first_ref, first_other_ref), (keep_ref, got_ref)):
            for part in range(2):
                lines = slice(part * own + start, part * own + start + step)
                term = one[lines, :].astype(F32) * two[lines, :].astype(F32)
                total = term if total is None else total + term
        image_ref[start : start + step, :] = total


def call(kernel, operands, outs, scratch=(), flops=0, name=None, scalars=1):
    moved = sum(math.prod(a.shape) * a.dtype.itemsize for a in operands)
    moved += sum(math.prod(a.shape) * a.dtype.itemsize for a in outs)
    return pl.pallas_call(
        kernel,
        out_shape=tuple(outs),
        in_specs=[SMEM] * scalars + [VMEM] * (len(operands) - scalars),
        out_specs=tuple(VMEM for _ in outs),
        scratch_shapes=list(scratch),
        compiler_params=pltpu.CompilerParams(vmem_limit_bytes=24 * 1024 * 1024),
        cost_estimate=pl.CostEstimate(flops=flops, bytes_accessed=moved, transcendentals=0),
        name=name,
    )(*operands)


def per_device(flight_fields, top_fields, slowness, ref_slowness, flight_blocks, top_block):
    slabs, chips = lax.axis_size("depth"), lax.axis_size("z")
    own, length_y = flight_fields.shape[3:]
    rows = 2 * own
    length_x = rows * chips
    half = length_y // 2
    block = half // chips
    even_x, odd_x, turned_x = cas_tables(length_x)
    even_y, odd_y, turned_y = cas_tables(length_y)
    depth, chip, core = (lax.axis_index(name) for name in ("depth", "z", "core"))
    place = jnp.stack([chip, core, (depth == slabs - 1).astype(jnp.int32)]).astype(jnp.int32)
    sign = 1.0 - 2.0 * core.astype(F32)

    def of(shape, dtype=BF16):
        return jax.ShapeDtypeStruct(shape, dtype)

    def other_core(value):
        return lax.ppermute(value, "core", [(0, 1), (1, 0)])

    def scalars(block_id, reference_s):
        angular = omega_top * (block_id.astype(F32) + 1.0) / NFREQ
        return jnp.stack([angular, reference_s, sign])

    def above(slab):
        return jnp.where(slab == 0, top_block[0], flight_blocks[jnp.maximum(slab - 1, 0)])

    def other_field(fields):
        taken = lax.dynamic_index_in_dim(fields, 1 - core, 0, keepdims=False)
        return other_core(taken.reshape(rows, length_y))

    fields = flight_fields.reshape(2 * rows, length_y)
    fields_other = other_field(flight_fields[0])

    below = lax.ppermute(
        ref_slowness, "depth", [((d + 1) % slabs, d) for d in range(slabs)]
    )
    target = (depth + 1 - core) % slabs
    first_scalars = scalars(flight_blocks[depth], ref_slowness[0])
    target_scalars = scalars(above(target), jnp.where(core == 1, ref_slowness[0], below[0]))
    second_scalars = scalars(above(depth), ref_slowness[0])

    cells = own * length_y

    def factors(scalar, odd):
        return call(
            functools.partial(factors_kernel, odd, length_y), (place, scalar),
            [of((length_x, block), F32)] * 2, flops=400 * cells, name="factors", scalars=2,
        )

    def phases(scalar):
        return call(
            phase_kernel, (place, scalar, slowness[0], slowness_other),
            [of((rows, length_y), F32)] * 2, flops=800 * cells, name="phases", scalars=2,
        )

    pieces_of = [of((rows, 2 * block))] * chips
    lines = (2 * rows, half)
    part = pltpu.VMEM(lines, BF16)
    flops = 2 * 2 * rows * half * half
    x_part = pltpu.VMEM((length_x, 2 * block), BF16)

    def exchange(pieces, moving=None):
        got = []
        for k, piece in zip(partners(chips), pieces):
            if k == 0 and moving is None:
                got.append(piece)
                continue
            pairs = []
            for d in range(slabs):
                for z in range(chips):
                    for c in range(2):
                        there = (d + 1) % slabs if c == moving else d
                        pairs.append(
                            ((d * chips + z) * 2 + c, (there * chips + (z ^ k)) * 2 + c)
                        )
            got.append(lax.ppermute(piece, ("depth", "z", "core"), pairs))
        return got

    def to_modes(odd):
        return call(
            functools.partial(to_modes_kernel, odd),
            (place, fields, fields_other, turned_y if odd else even_y),
            pieces_of, [part, part], flops, "to_modes",
        )

    def along_x(pieces, factor):
        return call(
            functools.partial(along_x_kernel, chips),
            (place, *factor, even_x, odd_x, turned_x, *pieces),
            pieces_of, [x_part, x_part], 2 * flops, "along_x",
        )

    def even_part(pieces):
        return call(
            even_part_kernel, (place, even_y, *pieces), [of(lines, F32)], [part], flops, "even_part"
        )[0]

    evens = exchange(to_modes(0))
    odds = exchange(to_modes(1))
    slowness_other = other_core(slowness[0])
    top_other = other_field(top_fields)
    evens = exchange(along_x(evens, factors(first_scalars, 0)))
    odds = exchange(along_x(odds, factors(first_scalars, 1)))
    *evens, folded, first_keep, first_give = call(
        functools.partial(turn_around_kernel, chips),
        (
            place, *phases(first_scalars), top_fields.reshape(2 * rows, length_y), top_other,
            even_y, odd_y, even_part(evens), *odds,
        ),
        pieces_of + [of(lines)] + [of((rows, length_y))] * 2,
        [part, pltpu.VMEM((2 * rows, length_y), BF16), part], 2 * flops, "turn_around",
    )
    evens = exchange(evens, 1)
    odds = exchange(
        call(odd_modes_kernel, (place, folded, turned_y), pieces_of, [part], flops, "odd_modes"), 1
    )
    first_got = other_core(first_give)
    evens = exchange(along_x(evens, factors(target_scalars, 0)), 0)
    odds = exchange(along_x(odds, factors(target_scalars, 1)), 0)
    second_phases = phases(second_scalars)
    first_part = even_part(evens)
    give, keep = [
        call(
            functools.partial(half_space_kernel, index),
            (place, *second_phases, odd_y, first_part, *odds),
            [of((rows, length_y))], [pltpu.VMEM((rows, half), BF16)], flops // 2, "half_space",
        )[0]
        for index in (1, 0)
    ]
    got = other_core(give)
    fields, image = call(
        finish_kernel, (place, first_keep, first_got, keep, got),
        [of((2 * rows, length_y)), of((own, length_y), F32)], flops=8 * cells, name="finish",
    )
    return image[None], fields.reshape(flight_fields.shape)


def passed_along(value, axis, steps):
    count = lax.axis_size(axis)
    leading, last = (max(0, -steps), min(count, count - steps))
    return lax.ppermute(value, axis, [(source, source + steps) for source in range(leading, last)])


def make_table(length):
    positions = jnp.arange(length, dtype=jnp.int32)
    product = positions[:, None] * positions[None, :] % length
    angles = product.astype(jnp.float32) * (2.0 * math.pi / length)
    scaling = 1.0 / math.sqrt(length)
    return (jnp.concatenate([jnp.cos(angles), jnp.sin(angles)], axis=1) * scaling).astype(
        jnp.bfloat16
    )


def wavenumber(positions, length):
    signed = jnp.where(positions < length // 2, positions, positions - length)
    return signed.astype(jnp.float32) * (2.0 * math.pi / length)


def mix(product, along, half_size, orient):
    cosine_part = lax.slice_in_dim(product, 0, half_size, axis=along)
    sine_part = lax.slice_in_dim(product, half_size, 2 * half_size, axis=along)
    real_part = cosine_part[:, 0] + orient * sine_part[:, 1]
    imag_part = cosine_part[:, 1] - orient * sine_part[:, 0]
    return jnp.stack([real_part, imag_part], axis=1)


def rotate(values, cosines, sine_vals):
    real_part = values[:, 0] * cosines - values[:, 1] * sine_vals
    imag_part = values[:, 0] * sine_vals + values[:, 1] * cosines
    return jnp.stack([real_part, imag_part], axis=1)


def spectral(angular, reference_s, wave_x, wave_y):
    quad = (angular * reference_s) ** 2 - wave_x * wave_x - wave_y * wave_y
    travel = jnp.sqrt(jnp.maximum(quad, 0.0)) * step_length
    damping = jnp.exp(-jnp.sqrt(jnp.maximum(-quad, 0.0)) * step_length)
    cosines = damping * jnp.cos(travel)
    sine_vals = damping * jnp.sin(travel)
    return (jnp.stack([cosines, cosines]), jnp.stack([sine_vals, -sine_vals]))


def propagate(fields, spec_cos, spec_sin, space_cos, space_sin, to_cols, to_rows, table_x, table_y):
    length_y = table_y.shape[0]
    length_x = table_x.shape[0]
    product = jnp.einsum("fcry,yk->fckr", fields, table_y, preferred_element_type=jnp.float32)
    first = mix(product, 2, length_y, 1.0).astype(jnp.bfloat16)
    columns = to_cols(first)
    product = jnp.dot(columns, table_x, preferred_element_type=jnp.float32)
    spectrum = mix(product, 3, length_x, 1.0)
    shifted = rotate(spectrum, spec_cos, spec_sin).astype(jnp.bfloat16)
    product = jnp.dot(shifted, table_x, preferred_element_type=jnp.float32)
    back_x = mix(product, 3, length_x, -1.0).astype(jnp.bfloat16)
    rows_back = to_rows(back_x)
    product = jnp.einsum("fckr,ky->fcry", rows_back, table_y, preferred_element_type=jnp.float32)
    space = mix(product, 3, length_y, -1.0)
    return rotate(space, space_cos, space_sin).astype(jnp.bfloat16)


def together_cols(values):
    return lax.all_to_all(values, "trans", split_axis=2, concat_axis=3, tiled=True)


def together_rows(values):
    return lax.all_to_all(values, "trans", split_axis=3, concat_axis=2, tiled=True)


def advance(fields, block_id, slowness, ref_slowness, table_x, table_y):
    length_x = table_x.shape[0]
    length_y = table_y.shape[0]
    trans_count = lax.axis_size("trans")
    local_ky = length_y // trans_count
    ky_rows = lax.axis_index("trans") * local_ky + jnp.arange(local_ky, dtype=jnp.int32)
    wave_y = wavenumber(ky_rows, length_y)[:, None]
    wave_x = wavenumber(jnp.arange(length_x, dtype=jnp.int32), length_x)[None, :]
    angular = omega_top * (block_id.astype(jnp.float32) + 1.0) / NFREQ
    reference_s = ref_slowness[0]
    spec_cos, spec_sin = spectral(angular, reference_s, wave_x, wave_y)
    rotation = angular * (slowness[0] - reference_s) * step_length
    cos_r = jnp.cos(rotation)
    sin_r = jnp.sin(rotation)
    space_cos = jnp.stack([cos_r, cos_r])
    space_sin = jnp.stack([sin_r, -sin_r])
    fields = propagate(
        fields,
        spec_cos,
        spec_sin,
        space_cos,
        space_sin,
        together_cols,
        together_rows,
        table_x,
        table_y,
    )
    values = fields.astype(jnp.float32)
    terms = [values[0, 0] * values[1, 0] + values[0, 1] * values[1, 1]]
    return (fields, jnp.stack(terms))


def general_per_device(flight_fields, top_fields, slowness, ref_slowness, flight_blocks, top_block):
    table_x = make_table(flight_fields.shape[3] * lax.axis_size("trans"))
    table_y = make_table(flight_fields.shape[4])
    depth_idx = lax.axis_index("depth")
    first_block = flight_blocks[depth_idx]
    above_block = flight_blocks[jnp.maximum(depth_idx - 1, 0)]
    second_block = jnp.where(depth_idx == 0, top_block[0], above_block)
    after_first, first_terms = advance(
        flight_fields[0], first_block, slowness, ref_slowness, table_x, table_y
    )
    handed = passed_along(after_first, "depth", 1)
    incoming = jnp.where(depth_idx == 0, top_fields, handed)
    after_second, second_terms = advance(
        incoming, second_block, slowness, ref_slowness, table_x, table_y
    )
    return (first_terms + second_terms, after_second[None])


def solution(mesh):
    slabs, count = mesh.shape["depth"], mesh.shape["trans"]
    chips = count // 2

    def mapped(body, over, trans):
        placed = (
            P("depth", None, None, trans, None),
            P(None, None, trans, None),
            P("depth", trans, None),
            P("depth"),
            P(),
            P(),
        )
        return jax.shard_map(
            body,
            mesh=over,
            in_specs=placed,
            out_specs=(P("depth", trans, None), P("depth", None, None, trans, None)),
            check_vma=False,
        )

    def run(*arrays):
        length_x, length_y = arrays[0].shape[3:]
        fits = count % 2 == 0 and chips & (chips - 1) == 0
        fits = fits and length_y % (256 * chips) == 0 and length_y % 512 == 0
        if not fits or length_x % (32 * chips) or length_x % 128:
            return mapped(general_per_device, mesh, "trans")(*arrays)
        cores = Mesh(mesh.devices.reshape(slabs, chips, 2), ("depth", "z", "core"))
        return mapped(per_device, cores, ("z", "core"))(*arrays)

    return run
```

```python
import functools
import math

import jax
import jax.numpy as jnp
import numpy as np
from jax import lax
from jax.experimental import pallas as pl
from jax.experimental.pallas import tpu as pltpu
from jax.sharding import Mesh, PartitionSpec as P

NFREQ = 256

omega_top = 4.0
step_length = 0.5

VMEM = pl.BlockSpec(memory_space=pltpu.VMEM)
SMEM = pl.BlockSpec(memory_space=pltpu.SMEM)
ANY = pl.BlockSpec(memory_space=pl.ANY)
F32 = jnp.float32
BF16 = jnp.bfloat16


def partners(count):
    return sorted(range(count), key=lambda k: (-k.bit_length(), k))


def cas_tables(length):
    positions = np.arange(length // 2, dtype=np.int64)
    quarter = length // 4

    def table(low):
        modes = np.concatenate([low, np.where(low == 0, length // 2, -low)])
        angles = (modes[:, None] * positions[None, :] % length) * (2.0 * math.pi / length)
        return ((np.cos(angles) + np.sin(angles)) / math.sqrt(length)).astype(jnp.bfloat16)

    both = [table(2 * positions[:quarter] + odd) for odd in (0, 1)]
    return [jnp.asarray(t) for one in both for t in (one, one.T.copy())]


def wave(index, length, odd):
    quarter = length // 4
    low = jnp.where(index < quarter, index, index - quarter)
    mode = 2 * low + odd
    if not odd:
        mode = jnp.where(index == quarter, length // 2, mode)
    return mode.astype(F32) * (2.0 * math.pi / length)


def dot(left, right):
    return jnp.dot(left, right, preferred_element_type=F32)


def fitted(function, degree):
    nodes = 2.1 * (1.0 + np.cos(math.pi * (np.arange(64) + 0.5) / 64))
    fit = np.polynomial.Chebyshev.fit(nodes, function(np.sqrt(nodes)), degree, domain=[0, 4.2])
    return [float(c) for c in fit.convert(kind=np.polynomial.Polynomial).coef]


COSINE = fitted(np.cos, 5)
SINE = fitted(lambda angle: np.sin(angle) / angle, 5)


def field_sign():
    return jnp.where(lax.axis_index("core") == 1, -1.0, 1.0)


def cos_sin(angle):
    square = angle * angle
    cosine = jnp.full_like(square, COSINE[-1])
    for coefficient in COSINE[-2::-1]:
        cosine = cosine * square + coefficient
    sine = jnp.full_like(square, SINE[-1])
    for coefficient in SINE[-2::-1]:
        sine = sine * square + coefficient
    return cosine, sine * angle


def factors_kernel(odd, length_y, stage, settings_ref, cos_ref, sin_ref):
    length_x, modes = cos_ref.shape
    quarter = length_x // 4
    angular, reference_s = settings_ref[2 * stage], settings_ref[2 * stage + 1]
    sign = field_sign()
    step = min(64, quarter)
    lane = lax.broadcasted_iota(jnp.int32, (step, modes), 1)
    line = lax.broadcasted_iota(jnp.int32, (step, modes), 0)
    wave_y = wave(lax.axis_index("z") * modes + lane, length_y, odd)
    constant = (angular * reference_s) ** 2 - wave_y * wave_y

    def work_out(wave_x, constant):
        quad = constant - wave_x * wave_x
        root = jnp.sqrt(jnp.abs(quad)) * step_length
        travels = quad > 0.0
        cosine, sine = cos_sin(jnp.where(travels, root, 0.0))
        damping = jnp.exp(jnp.where(travels, 0.0, -root))
        return damping * cosine, (sign * damping) * sine

    for x_odd in range(2):
        for start in range(0, quarter, step):
            values = work_out(wave(start + line, length_x, x_odd), constant)
            for half in range(2):
                at = (2 * x_odd + half) * quarter + start
                cos_ref[at : at + step, :], sin_ref[at : at + step, :] = values
    values = work_out(wave(quarter + line[:8], length_x, 0), constant[:8])
    cos_ref[quarter : quarter + 8, :], sin_ref[quarter : quarter + 8, :] = values


def phase_kernel(stage, settings_ref, mine_ref, other_ref, cos_ref, sin_ref):
    angular, reference_s = settings_ref[2 * stage], settings_ref[2 * stage + 1]
    sign = field_sign()
    rows = mine_ref.shape[0]
    step = 8
    for index, slowness in enumerate((mine_ref, other_ref)):
        start = (lax.axis_index("core") ^ index) * rows

        @pl.loop(0, rows // step)
        def _(chunk):
            there = pl.ds(pl.multiple_of(start + chunk * step, step), step)
            here = pl.ds(pl.multiple_of(chunk * step, step), step)
            cosine, sine = cos_sin(angular * (slowness[here, :] - reference_s) * step_length)
            cos_ref[there, :] = cosine
            sin_ref[there, :] = sign * sine


def rows_of(start, size):
    return pl.ds(pl.multiple_of(start, size), size)


def split_modes(here, whole, outs):
    rows, width = outs[0].shape
    block = width // 2
    for k, out in zip(partners(len(outs)), outs):
        columns = rows_of((here ^ k) * block, block)
        for part in range(2):
            out[:, part * block : (part + 1) * block] = whole[
                part * rows : (part + 1) * rows, columns
            ]


def join_modes(here, pieces, whole, lines=None):
    rows, width = pieces[0].shape
    block = width // 2
    size = rows if lines is None else lines.size
    for k, piece in zip(partners(len(pieces)), pieces):
        columns = rows_of((here ^ k) * block, block)
        for part in range(2):
            whole[part * size : (part + 1) * size, columns] = piece[
                slice(None) if lines is None else lines, part * block : (part + 1) * block
            ]


def to_modes_kernel(odd, fields_ref, other_ref, table_ref, *refs):
    outs, (folded, modes) = refs[:-2], refs[-2:]
    rows = other_ref.shape[0] // 4
    half = table_ref.shape[0]
    core = lax.axis_index("core")
    for part in range(2):
        mine = rows_of((2 * core + part) * rows, rows)
        for index, source in enumerate((fields_ref, other_ref)):
            low, high = source[mine, :half], source[mine, half:]
            there = rows_of(2 * part * rows + (core ^ index) * rows, rows)
            folded[there, :] = low - high if odd else low + high
    modes[...] = dot(folded[...], table_ref[...]).astype(BF16)
    split_modes(lax.axis_index("z"), modes, outs)


def along_x_kernel(
    count, cos_ref, sin_ref, even_ref, even_t_ref, odd_ref, odd_t_ref, *refs
):
    pieces, outs = refs[:count], refs[count : 2 * count]
    held, shifted = refs[2 * count :]
    here = lax.axis_index("z")
    rows, width = outs[0].shape
    block = width // 2
    for k, piece in zip(partners(count), pieces):
        held[rows_of((here ^ k) * rows, rows), :] = piece[...]
    half = even_ref.shape[0]
    low, high = held[:half, :], held[half:, :]
    for part, table, values in ((0, even_ref, low + high), (1, odd_ref, low - high)):
        lines = slice(part * half, (part + 1) * half)
        spectrum = dot(table[...], values)
        real, imag = spectrum[:, :block], spectrum[:, block:]
        cosine, sine = cos_ref[lines, :], sin_ref[lines, :]
        shifted[lines, :block] = (real * cosine - imag * sine).astype(BF16)
        shifted[lines, block:] = (real * sine + imag * cosine).astype(BF16)
    first = dot(even_t_ref[...], shifted[:half, :])
    second = dot(odd_t_ref[...], shifted[half:, :])
    held[:half, :] = (first + second).astype(BF16)
    held[half:, :] = (first - second).astype(BF16)
    for k, out in zip(partners(count), outs):
        out[...] = held[rows_of((here ^ k) * rows, rows), :]


def even_part_kernel(table_ref, *refs):
    pieces, (out_ref, modes) = refs[:-2], refs[-2:]
    join_modes(lax.axis_index("z"), pieces, modes)
    out_ref[...] = dot(modes[...], table_ref[...])


def turned(real, imag, cosine, sine):
    return (real * cosine - imag * sine).astype(BF16), (real * sine + imag * cosine).astype(BF16)


def turn_around_kernel(
    count, cos_ref, sin_ref, top_ref, top_other_ref, even_t_ref, odd_ref, part_ref, *refs
):
    pieces, outs = refs[:count], refs[count : 2 * count]
    folded_ref, keep_ref, give_ref, modes, space, sums = refs[2 * count :]
    here, core = lax.axis_index("z"), lax.axis_index("core")
    rows = pieces[0].shape[0]
    own = rows // 2
    half = odd_ref.shape[0]
    join_modes(here, pieces, modes)
    step = 256
    for start in range(0, half, step):
        columns = slice(start, start + step)
        second = dot(modes[...], odd_ref[:, columns])
        first = part_ref[:, columns]
        for values, at in ((first + second, start), (first - second, start + half)):
            lanes = slice(at, at + step)
            real, imag = turned(values[:rows], values[rows:], cos_ref[:, lanes], sin_ref[:, lanes])
            space[:rows, lanes] = real
            space[rows:, lanes] = imag
    for index, out in enumerate((keep_ref, give_ref)):
        for part in range(2):
            out[part * own : (part + 1) * own, :] = space[
                rows_of(part * rows + (core ^ index) * own, own), :
            ]

    @pl.when(lax.axis_index("depth") == lax.axis_size("depth") - 1)
    def _():
        for part in range(2):
            space[rows_of(part * rows + core * own, own), :] = top_ref[
                rows_of((2 * core + part) * own, own), :
            ]
            space[rows_of(part * rows + (core ^ 1) * own, own), :] = top_other_ref[
                rows_of((2 * core + part) * own, own), :
            ]

    sums[...] = space[:, :half] + space[:, half:]
    folded_ref[...] = space[:, :half] - space[:, half:]
    modes[...] = dot(sums[...], even_t_ref[...]).astype(BF16)
    split_modes(here, modes, outs)


def odd_modes_kernel(folded_ref, table_ref, *refs):
    outs, modes = refs[:-1], refs[-1]
    modes[...] = dot(folded_ref[...], table_ref[...]).astype(BF16)
    split_modes(lax.axis_index("z"), modes, outs)


def half_space_kernel(index, cos_ref, sin_ref, odd_ref, part_ref, *refs):
    pieces, (out_ref, modes) = refs[:-2], refs[-2:]
    rows = pieces[0].shape[0]
    own = rows // 2
    half = odd_ref.shape[0]
    offset = (lax.axis_index("core") ^ index) * own
    lines = rows_of(offset, own)
    join_modes(lax.axis_index("z"), pieces, modes, lines)
    step = 256
    for start in range(0, half, step):
        columns = slice(start, start + step)
        second = dot(modes[...], odd_ref[:, columns])
        for sign, at in ((1.0, start), (-1.0, start + half)):
            lanes = slice(at, at + step)
            real, imag = [
                part_ref[rows_of(part * rows + offset, own), columns]
                + sign * second[part * own : (part + 1) * own]
                for part in range(2)
            ]
            out_ref[:own, lanes], out_ref[own:, lanes] = turned(
                real, imag, cos_ref[lines, lanes], sin_ref[lines, lanes]
            )


def finish_kernel(first_ref, first_other_ref, keep_ref, got_ref, fields_ref, image_ref):
    rows = keep_ref.shape[0]
    own = rows // 2
    core = lax.axis_index("core")
    fields_ref[rows_of(core * rows, rows), :] = keep_ref[...]
    fields_ref[rows_of((core ^ 1) * rows, rows), :] = got_ref[...]
    step = 16
    for start in range(0, own, step):
        total = None
        for one, two in ((first_ref, first_other_ref), (keep_ref, got_ref)):
            for part in range(2):
                lines = slice(part * own + start, part * own + start + step)
                term = one[lines, :].astype(F32) * two[lines, :].astype(F32)
                total = term if total is None else total + term
        image_ref[start : start + step, :] = total


def after(count, kernel, *refs):
    return kernel(*refs[count:])


def call(kernel, operands, outs, scratch=(), flops=0, name=None, scalars=0, behind=()):
    moved = sum(math.prod(a.shape) * a.dtype.itemsize for a in operands)
    moved += sum(math.prod(a.shape) * a.dtype.itemsize for a in outs)
    return pl.pallas_call(
        functools.partial(after, len(behind), kernel),
        out_shape=tuple(outs),
        in_specs=[ANY] * len(behind) + [SMEM] * scalars + [VMEM] * (len(operands) - scalars),
        out_specs=tuple(VMEM for _ in outs),
        scratch_shapes=list(scratch),
        compiler_params=pltpu.CompilerParams(vmem_limit_bytes=24 * 1024 * 1024),
        cost_estimate=pl.CostEstimate(flops=flops, bytes_accessed=moved, transcendentals=0),
        name=name,
    )(*behind, *operands)


def per_device(flight_fields, top_fields, slowness, ref_slowness, flight_blocks, top_block):
    slabs, chips = lax.axis_size("depth"), lax.axis_size("z")
    own, length_y = flight_fields.shape[3:]
    rows = 2 * own
    length_x = rows * chips
    half = length_y // 2
    block = half // chips
    cells = own * length_y
    tables_x = cas_tables(length_x)
    even_y, even_y_t, odd_y, odd_y_t = tables_x if length_x == length_y else cas_tables(length_y)

    def of(shape, dtype=BF16):
        return jax.ShapeDtypeStruct(shape, dtype)

    def other_core(value):
        return lax.ppermute(value, "core", [(0, 1), (1, 0)])

    fields = flight_fields.reshape(2 * rows, length_y)
    top = top_fields.reshape(2 * rows, length_y)
    mine = slowness[0]
    fields_other, top_other, other = other_core(fields), other_core(top), other_core(mine)
    below = lax.ppermute(ref_slowness, "depth", [((d + 1) % slabs, d) for d in range(slabs)])

    depth = lax.axis_index("depth")

    def angular(block_id):
        return omega_top * (block_id.astype(F32) + 1.0) / NFREQ

    second = jnp.where(depth == 0, top_block[0], flight_blocks[jnp.maximum(depth - 1, 0)])
    odd_second = jnp.where(depth == slabs - 1, top_block[0], flight_blocks[depth])
    settings = jnp.stack([
        angular(flight_blocks[depth]), ref_slowness[0],
        angular(second), ref_slowness[0],
        angular(odd_second), below[0],
    ])

    def factors(stage, odd, behind):
        return call(
            functools.partial(factors_kernel, odd, length_y, stage), (settings,),
            [of((length_x, block), F32)] * 2, flops=400 * cells, name="factors", scalars=1,
            behind=behind,
        )

    def phases(stage, behind):
        return call(
            functools.partial(phase_kernel, stage), (settings, mine, other),
            [of((rows, length_y), F32)] * 2, flops=800 * cells, name="phases", scalars=1,
            behind=behind,
        )

    pieces_of = [of((rows, 2 * block))] * chips
    lines = (2 * rows, half)
    part = pltpu.VMEM(lines, BF16)
    flops = 2 * 2 * rows * half * half
    x_part = pltpu.VMEM((length_x, 2 * block), BF16)

    def exchange(pieces, down=0):
        got = []
        for k, piece in zip(partners(chips), pieces):
            if down:
                pairs = [
                    (d * chips + z, (d + down) % slabs * chips + (z ^ k))
                    for d in range(slabs)
                    for z in range(chips)
                ]
                got.append(lax.ppermute(piece, ("depth", "z"), pairs))
            else:
                pairs = [(z, z ^ k) for z in range(chips)]
                got.append(lax.ppermute(piece, "z", pairs) if k else piece)
        return got

    def to_modes(odd, behind=()):
        return call(
            functools.partial(to_modes_kernel, odd),
            (fields, fields_other, odd_y_t if odd else even_y_t),
            pieces_of, [part, part], flops, "to_modes", behind=behind,
        )

    def along_x(pieces, factor, behind=()):
        return call(
            functools.partial(along_x_kernel, chips), (*factor, *tables_x, *pieces),
            pieces_of, [x_part, x_part], 2 * flops, "along_x", behind=behind,
        )

    def even_part(pieces):
        return call(
            even_part_kernel, (even_y, *pieces), [of(lines, F32)], [part], flops, "even_part"
        )[0]

    evens = to_modes(0)
    odds = to_modes(1, (top_other, other, below))
    ready = (odds[-1],)
    even_factors, odd_factors = factors(0, 0, ready), factors(0, 1, ready)
    first_phases = phases(0, ready)
    evens, odds = exchange(evens), exchange(odds)
    evens = exchange(along_x(evens, even_factors, (odd_factors[0], first_phases[0])))
    odds = exchange(along_x(odds, odd_factors))
    *evens, folded, first_keep, first_give = call(
        functools.partial(turn_around_kernel, chips),
        (*first_phases, top, top_other, even_y_t, odd_y, even_part(evens), *odds),
        pieces_of + [of(lines)] + [of((rows, length_y))] * 2,
        [part, pltpu.VMEM((2 * rows, length_y), BF16), part], 2 * flops, "turn_around",
    )
    odds = call(odd_modes_kernel, (folded, odd_y_t), pieces_of, [part], flops, "odd_modes")
    ready = (odds[-1],)
    even_factors, odd_factors = factors(1, 0, ready), factors(2, 1, ready)
    second_phases = phases(1, ready)
    evens, odds = exchange(evens, 1), exchange(odds)
    first_got = other_core(first_give)
    evens = exchange(along_x(evens, even_factors, (odd_factors[0], second_phases[0])))
    odds = exchange(along_x(odds, odd_factors), 1)
    first_part = even_part(evens)
    give, keep = [
        call(
            functools.partial(half_space_kernel, index),
            (*second_phases, odd_y, first_part, *odds),
            [of((rows, length_y))], [pltpu.VMEM((rows, half), BF16)], flops // 2, "half_space",
        )[0]
        for index in (1, 0)
    ]
    got = other_core(give)
    fields, image = call(
        finish_kernel, (first_keep, first_got, keep, got),
        [of((2 * rows, length_y)), of((own, length_y), F32)], flops=8 * cells, name="finish",
    )
    return image[None], fields.reshape(flight_fields.shape)


def passed_along(value, axis, steps):
    count = lax.axis_size(axis)
    leading, last = (max(0, -steps), min(count, count - steps))
    return lax.ppermute(value, axis, [(source, source + steps) for source in range(leading, last)])


def make_table(length):
    positions = jnp.arange(length, dtype=jnp.int32)
    product = positions[:, None] * positions[None, :] % length
    angles = product.astype(jnp.float32) * (2.0 * math.pi / length)
    scaling = 1.0 / math.sqrt(length)
    return (jnp.concatenate([jnp.cos(angles), jnp.sin(angles)], axis=1) * scaling).astype(
        jnp.bfloat16
    )


def wavenumber(positions, length):
    signed = jnp.where(positions < length // 2, positions, positions - length)
    return signed.astype(jnp.float32) * (2.0 * math.pi / length)


def mix(product, along, half_size, orient):
    cosine_part = lax.slice_in_dim(product, 0, half_size, axis=along)
    sine_part = lax.slice_in_dim(product, half_size, 2 * half_size, axis=along)
    real_part = cosine_part[:, 0] + orient * sine_part[:, 1]
    imag_part = cosine_part[:, 1] - orient * sine_part[:, 0]
    return jnp.stack([real_part, imag_part], axis=1)


def rotate(values, cosines, sine_vals):
    real_part = values[:, 0] * cosines - values[:, 1] * sine_vals
    imag_part = values[:, 0] * sine_vals + values[:, 1] * cosines
    return jnp.stack([real_part, imag_part], axis=1)


def spectral(angular, reference_s, wave_x, wave_y):
    quad = (angular * reference_s) ** 2 - wave_x * wave_x - wave_y * wave_y
    travel = jnp.sqrt(jnp.maximum(quad, 0.0)) * step_length
    damping = jnp.exp(-jnp.sqrt(jnp.maximum(-quad, 0.0)) * step_length)
    cosines = damping * jnp.cos(travel)
    sine_vals = damping * jnp.sin(travel)
    return (jnp.stack([cosines, cosines]), jnp.stack([sine_vals, -sine_vals]))


def propagate(fields, spec_cos, spec_sin, space_cos, space_sin, to_cols, to_rows, table_x, table_y):
    length_y = table_y.shape[0]
    length_x = table_x.shape[0]
    product = jnp.einsum("fcry,yk->fckr", fields, table_y, preferred_element_type=jnp.float32)
    first = mix(product, 2, length_y, 1.0).astype(jnp.bfloat16)
    columns = to_cols(first)
    product = jnp.dot(columns, table_x, preferred_element_type=jnp.float32)
    spectrum = mix(product, 3, length_x, 1.0)
    shifted = rotate(spectrum, spec_cos, spec_sin).astype(jnp.bfloat16)
    product = jnp.dot(shifted, table_x, preferred_element_type=jnp.float32)
    back_x = mix(product, 3, length_x, -1.0).astype(jnp.bfloat16)
    rows_back = to_rows(back_x)
    product = jnp.einsum("fckr,ky->fcry", rows_back, table_y, preferred_element_type=jnp.float32)
    space = mix(product, 3, length_y, -1.0)
    return rotate(space, space_cos, space_sin).astype(jnp.bfloat16)


def together_cols(values):
    return lax.all_to_all(values, "trans", split_axis=2, concat_axis=3, tiled=True)


def together_rows(values):
    return lax.all_to_all(values, "trans", split_axis=3, concat_axis=2, tiled=True)


def advance(fields, block_id, slowness, ref_slowness, table_x, table_y):
    length_x = table_x.shape[0]
    length_y = table_y.shape[0]
    trans_count = lax.axis_size("trans")
    local_ky = length_y // trans_count
    ky_rows = lax.axis_index("trans") * local_ky + jnp.arange(local_ky, dtype=jnp.int32)
    wave_y = wavenumber(ky_rows, length_y)[:, None]
    wave_x = wavenumber(jnp.arange(length_x, dtype=jnp.int32), length_x)[None, :]
    angular = omega_top * (block_id.astype(jnp.float32) + 1.0) / NFREQ
    reference_s = ref_slowness[0]
    spec_cos, spec_sin = spectral(angular, reference_s, wave_x, wave_y)
    rotation = angular * (slowness[0] - reference_s) * step_length
    cos_r = jnp.cos(rotation)
    sin_r = jnp.sin(rotation)
    space_cos = jnp.stack([cos_r, cos_r])
    space_sin = jnp.stack([sin_r, -sin_r])
    fields = propagate(
        fields,
        spec_cos,
        spec_sin,
        space_cos,
        space_sin,
        together_cols,
        together_rows,
        table_x,
        table_y,
    )
    values = fields.astype(jnp.float32)
    terms = [values[0, 0] * values[1, 0] + values[0, 1] * values[1, 1]]
    return (fields, jnp.stack(terms))


def general_per_device(flight_fields, top_fields, slowness, ref_slowness, flight_blocks, top_block):
    table_x = make_table(flight_fields.shape[3] * lax.axis_size("trans"))
    table_y = make_table(flight_fields.shape[4])
    depth_idx = lax.axis_index("depth")
    first_block = flight_blocks[depth_idx]
    above_block = flight_blocks[jnp.maximum(depth_idx - 1, 0)]
    second_block = jnp.where(depth_idx == 0, top_block[0], above_block)
    after_first, first_terms = advance(
        flight_fields[0], first_block, slowness, ref_slowness, table_x, table_y
    )
    handed = passed_along(after_first, "depth", 1)
    incoming = jnp.where(depth_idx == 0, top_fields, handed)
    after_second, second_terms = advance(
        incoming, second_block, slowness, ref_slowness, table_x, table_y
    )
    return (first_terms + second_terms, after_second[None])


def solution(mesh):
    slabs, count = mesh.shape["depth"], mesh.shape["trans"]
    chips = count // 2

    def mapped(body, over, trans):
        placed = (
            P("depth", None, None, trans, None),
            P(None, None, trans, None),
            P("depth", trans, None),
            P("depth"),
            P(),
            P(),
        )
        return jax.shard_map(
            body,
            mesh=over,
            in_specs=placed,
            out_specs=(P("depth", trans, None), P("depth", None, None, trans, None)),
            check_vma=False,
        )

    def run(*arrays):
        length_x, length_y = arrays[0].shape[3:]
        fits = count % 2 == 0 and chips & (chips - 1) == 0
        fits = fits and length_y % (256 * chips) == 0 and length_y % 512 == 0
        if not fits or length_x % (32 * chips) or length_x % 128:
            return mapped(general_per_device, mesh, "trans")(*arrays)
        cores = Mesh(mesh.devices.reshape(slabs, chips, 2), ("depth", "z", "core"))
        return mapped(per_device, cores, ("z", "core"))(*arrays)

    return run
```

```python
import functools
import math

import jax
import jax.numpy as jnp
import numpy as np
from jax import lax
from jax.experimental import pallas as pl
from jax.experimental.pallas import tpu as pltpu
from jax.sharding import Mesh, PartitionSpec as P

NFREQ = 256

omega_top = 4.0
step_length = 0.5

VMEM = pl.BlockSpec(memory_space=pltpu.VMEM)
SMEM = pl.BlockSpec(memory_space=pltpu.SMEM)
ANY = pl.BlockSpec(memory_space=pl.ANY)
HBM = pl.BlockSpec(memory_space=pltpu.HBM)
F32 = jnp.float32
BF16 = jnp.bfloat16


def partners(count):
    return sorted(range(count), key=lambda k: (-k.bit_length(), k))


def cas_tables(length):
    positions = np.arange(length // 2, dtype=np.int64)
    quarter = length // 4

    def table(low):
        modes = np.concatenate([low, np.where(low == 0, length // 2, -low)])
        angles = (modes[:, None] * positions[None, :] % length) * (2.0 * math.pi / length)
        return ((np.cos(angles) + np.sin(angles)) / math.sqrt(length)).astype(jnp.bfloat16)

    both = [table(2 * positions[:quarter] + odd) for odd in (0, 1)]
    return [jnp.asarray(t) for one in both for t in (one, one.T.copy())]


def wave(index, length, odd):
    quarter = length // 4
    low = jnp.where(index < quarter, index, index - quarter)
    mode = 2 * low + odd
    if not odd:
        mode = jnp.where(index == quarter, length // 2, mode)
    return mode.astype(F32) * (2.0 * math.pi / length)


def dot(left, right):
    return jnp.dot(left, right, preferred_element_type=F32)


def fitted(function, degree):
    nodes = 2.1 * (1.0 + np.cos(math.pi * (np.arange(64) + 0.5) / 64))
    fit = np.polynomial.Chebyshev.fit(nodes, function(np.sqrt(nodes)), degree, domain=[0, 4.2])
    return [float(c) for c in fit.convert(kind=np.polynomial.Polynomial).coef]


COSINE = fitted(np.cos, 5)
SINE = fitted(lambda angle: np.sin(angle) / angle, 5)


def field_sign():
    return jnp.where(lax.axis_index("core") == 1, -1.0, 1.0)


def cos_sin(angle):
    square = angle * angle
    cosine = jnp.full_like(square, COSINE[-1])
    for coefficient in COSINE[-2::-1]:
        cosine = cosine * square + coefficient
    sine = jnp.full_like(square, SINE[-1])
    for coefficient in SINE[-2::-1]:
        sine = sine * square + coefficient
    return cosine, sine * angle


def factors_kernel(odd, length_y, stage, settings_ref, cos_ref, sin_ref):
    length_x, modes = cos_ref.shape
    quarter = length_x // 4
    angular, reference_s = settings_ref[2 * stage], settings_ref[2 * stage + 1]
    sign = field_sign()
    step = min(64, quarter)
    lane = lax.broadcasted_iota(jnp.int32, (step, modes), 1)
    line = lax.broadcasted_iota(jnp.int32, (step, modes), 0)
    wave_y = wave(lax.axis_index("z") * modes + lane, length_y, odd)
    constant = (angular * reference_s) ** 2 - wave_y * wave_y

    def work_out(wave_x, constant):
        quad = constant - wave_x * wave_x
        root = jnp.sqrt(jnp.abs(quad)) * step_length
        travels = quad > 0.0
        cosine, sine = cos_sin(jnp.where(travels, root, 0.0))
        damping = jnp.exp(jnp.where(travels, 0.0, -root))
        return damping * cosine, (sign * damping) * sine

    for x_odd in range(2):
        for start in range(0, quarter, step):
            values = work_out(wave(start + line, length_x, x_odd), constant)
            for half in range(2):
                at = (2 * x_odd + half) * quarter + start
                cos_ref[at : at + step, :], sin_ref[at : at + step, :] = values
    values = work_out(wave(quarter + line[:8], length_x, 0), constant[:8])
    cos_ref[quarter : quarter + 8, :], sin_ref[quarter : quarter + 8, :] = values


def phase_kernel(stage, settings_ref, mine_ref, other_ref, cos_ref, sin_ref):
    angular, reference_s = settings_ref[2 * stage], settings_ref[2 * stage + 1]
    sign = field_sign()
    rows = mine_ref.shape[0]
    step = 8
    for index, slowness in enumerate((mine_ref, other_ref)):
        start = (lax.axis_index("core") ^ index) * rows

        @pl.loop(0, rows // step)
        def _(chunk):
            there = pl.ds(pl.multiple_of(start + chunk * step, step), step)
            here = pl.ds(pl.multiple_of(chunk * step, step), step)
            cosine, sine = cos_sin(angular * (slowness[here, :] - reference_s) * step_length)
            cos_ref[there, :] = cosine
            sin_ref[there, :] = sign * sine


def rows_of(start, size):
    return pl.ds(pl.multiple_of(start, size), size)


def split_modes(here, whole, outs):
    rows, width = outs[0].shape
    block = width // 2
    for k, out in zip(partners(len(outs)), outs):
        columns = rows_of((here ^ k) * block, block)
        for part in range(2):
            out[:, part * block : (part + 1) * block] = whole[
                part * rows : (part + 1) * rows, columns
            ]


def join_modes(here, pieces, whole, lines=None):
    rows, width = pieces[0].shape
    block = width // 2
    size = rows if lines is None else lines.size
    for k, piece in zip(partners(len(pieces)), pieces):
        columns = rows_of((here ^ k) * block, block)
        for part in range(2):
            whole[part * size : (part + 1) * size, columns] = piece[
                slice(None) if lines is None else lines, part * block : (part + 1) * block
            ]


def own_modes_kernel(fields_ref, even_ref, odd_ref, evens_ref, odds_ref, held, tables, sems):
    rows, half = evens_ref.shape
    copies = [
        pltpu.make_async_copy(
            fields_ref.at[rows_of(lax.axis_index("core") * rows, rows), :], held, sems.at[0]
        ),
        pltpu.make_async_copy(even_ref, tables.at[0], sems.at[1]),
        pltpu.make_async_copy(odd_ref, tables.at[1], sems.at[2]),
    ]
    for copy in copies:
        copy.start()
    copies[0].wait()
    low, high = held[:, :half], held[:, half:]
    copies[1].wait()
    evens_ref[...] = dot(low + high, tables[0]).astype(BF16)
    copies[2].wait()
    odds_ref[...] = dot(low - high, tables[1]).astype(BF16)


def to_modes_kernel(odd, other_ref, own_ref, table_ref, *refs):
    outs, modes = refs[:-1], refs[-1]
    rows, half = own_ref.shape
    own = rows // 2
    core = lax.axis_index("core")
    theirs = rows_of(core * rows, rows)
    low, high = other_ref[theirs, :half], other_ref[theirs, half:]
    modes[...] = dot(low - high if odd else low + high, table_ref[...]).astype(BF16)
    block = half // len(outs)
    for k, out in zip(partners(len(outs)), outs):
        columns = rows_of((lax.axis_index("z") ^ k) * block, block)
        for part in range(2):
            lanes = slice(part * block, (part + 1) * block)
            lines = slice(part * own, (part + 1) * own)
            out[rows_of(core * own, own), lanes] = own_ref[lines, columns]
            out[rows_of((core ^ 1) * own, own), lanes] = modes[lines, columns]


def odd_to_modes_kernel(blocks_ref, top_block_ref, reference_ref, *refs):
    settings_ref = refs[-2]
    depth = lax.axis_index("depth")
    above = blocks_ref[jnp.maximum(depth - 1, 0)]
    second = jnp.where(depth == 0, top_block_ref[0], above)
    for index, block in enumerate((blocks_ref[depth], second)):
        settings_ref[2 * index] = omega_top * (block.astype(F32) + 1.0) / NFREQ
        settings_ref[2 * index + 1] = reference_ref[0]
    to_modes_kernel(1, *refs[:-2], refs[-1])


def along_x_kernel(
    count, cos_ref, sin_ref, even_ref, even_t_ref, odd_ref, odd_t_ref, *refs
):
    pieces, outs = refs[:count], refs[count : 2 * count]
    held, shifted = refs[2 * count :]
    here = lax.axis_index("z")
    rows, width = outs[0].shape
    block = width // 2
    for k, piece in zip(partners(count), pieces):
        held[rows_of((here ^ k) * rows, rows), :] = piece[...]
    half = even_ref.shape[0]
    low, high = held[:half, :], held[half:, :]
    for part, table, values in ((0, even_ref, low + high), (1, odd_ref, low - high)):
        lines = slice(part * half, (part + 1) * half)
        spectrum = dot(table[...], values)
        real, imag = spectrum[:, :block], spectrum[:, block:]
        cosine, sine = cos_ref[lines, :], sin_ref[lines, :]
        shifted[lines, :block] = (real * cosine - imag * sine).astype(BF16)
        shifted[lines, block:] = (real * sine + imag * cosine).astype(BF16)
    first = dot(even_t_ref[...], shifted[:half, :])
    second = dot(odd_t_ref[...], shifted[half:, :])
    held[:half, :] = (first + second).astype(BF16)
    held[half:, :] = (first - second).astype(BF16)
    for k, out in zip(partners(count), outs):
        out[...] = held[rows_of((here ^ k) * rows, rows), :]


def even_part_kernel(table_ref, *refs):
    pieces, (out_ref, modes) = refs[:-2], refs[-2:]
    join_modes(lax.axis_index("z"), pieces, modes)
    out_ref[...] = dot(modes[...], table_ref[...])


def turned(real, imag, cosine, sine):
    return (real * cosine - imag * sine).astype(BF16), (real * sine + imag * cosine).astype(BF16)


def turn_around_kernel(
    count, cos_ref, sin_ref, top_ref, top_other_ref, even_t_ref, odd_ref, part_ref, *refs
):
    pieces, outs = refs[:count], refs[count : 2 * count]
    folded_ref, both_ref, modes, sums = refs[2 * count :]
    here, core = lax.axis_index("z"), lax.axis_index("core")
    rows = pieces[0].shape[0]
    own = rows // 2
    half = odd_ref.shape[0]
    join_modes(here, pieces, modes)
    step = 256
    for start in range(0, half, step):
        columns = slice(start, start + step)
        second = dot(modes[...], odd_ref[:, columns])
        first = part_ref[:, columns]
        stepped = []
        for values, at in ((first + second, start), (first - second, start + half)):
            lanes = slice(at, at + step)
            fields = turned(values[:rows], values[rows:], cos_ref[:, lanes], sin_ref[:, lanes])
            stepped.append(fields)
            for index in range(2):
                for part, field in enumerate(fields):
                    there = (2 * index + part) * own
                    both_ref[there : there + own, lanes] = field[index * own : (index + 1) * own]
        for part in range(2):
            lines = slice(part * rows, (part + 1) * rows)
            sums[lines, columns] = stepped[0][part] + stepped[1][part]
            folded_ref[lines, columns] = stepped[0][part] - stepped[1][part]

    @pl.when(lax.axis_index("depth") == lax.axis_size("depth") - 1)
    def _():
        for index, source in enumerate((top_ref, top_other_ref)):
            for part in range(2):
                lines = rows_of((2 * core + part) * own, own)
                low, high = source[lines, :half], source[lines, half:]
                there = rows_of(part * rows + (core ^ index) * own, own)
                sums[there, :] = low + high
                folded_ref[there, :] = low - high

    modes[...] = dot(sums[...], even_t_ref[...]).astype(BF16)
    split_modes(here, modes, outs)


def odd_modes_kernel(folded_ref, table_ref, *refs):
    outs, modes = refs[:-1], refs[-1]
    modes[...] = dot(folded_ref[...], table_ref[...]).astype(BF16)
    split_modes(lax.axis_index("z"), modes, outs)


def half_space_kernel(index, cos_ref, sin_ref, odd_ref, part_ref, *refs):
    pieces, (out_ref, modes) = refs[:-2], refs[-2:]
    rows = pieces[0].shape[0]
    own = rows // 2
    half = odd_ref.shape[0]
    offset = (lax.axis_index("core") ^ index) * own
    lines = rows_of(offset, own)
    join_modes(lax.axis_index("z"), pieces, modes, lines)
    step = 256
    for start in range(0, half, step):
        columns = slice(start, start + step)
        second = dot(modes[...], odd_ref[:, columns])
        for sign, at in ((1.0, start), (-1.0, start + half)):
            lanes = slice(at, at + step)
            real, imag = [
                part_ref[rows_of(part * rows + offset, own), columns]
                + sign * second[part * own : (part + 1) * own]
                for part in range(2)
            ]
            out_ref[:own, lanes], out_ref[own:, lanes] = turned(
                real, imag, cos_ref[lines, lanes], sin_ref[lines, lanes]
            )


def other_rows_kernel(both_ref, out_ref):
    rows = out_ref.shape[0]
    out_ref[...] = both_ref[rows_of((lax.axis_index("core") ^ 1) * rows, rows), :]


def finish_kernel(first_ref, first_other_ref, keep_ref, got_ref, fields_ref, image_ref):
    rows = keep_ref.shape[0]
    own = rows // 2
    core = lax.axis_index("core")
    fields_ref[rows_of(core * rows, rows), :] = keep_ref[...]
    fields_ref[rows_of((core ^ 1) * rows, rows), :] = got_ref[...]
    step = 16
    for start in range(0, own, step):
        total = None
        for part in range(2):
            lines = slice(part * own + start, part * own + start + step)
            mine = rows_of(core * rows + part * own + start, step)
            for one, two in (
                (first_ref[mine, :], first_other_ref[lines, :]),
                (keep_ref[lines, :], got_ref[lines, :]),
            ):
                term = one.astype(F32) * two.astype(F32)
                total = term if total is None else total + term
        image_ref[start : start + step, :] = total


def after(count, kernel, *refs):
    return kernel(*refs[count:])


def call(
    kernel, operands, outs, scratch=(), flops=0, name=None, scalars=0, behind=(), ins=None, puts=None,
    grant=24,
):
    moved = sum(math.prod(a.shape) * a.dtype.itemsize for a in operands)
    moved += sum(math.prod(a.shape) * a.dtype.itemsize for a in outs)
    return pl.pallas_call(
        functools.partial(after, len(behind), kernel),
        out_shape=tuple(outs),
        in_specs=[ANY] * len(behind)
        + (ins or [SMEM] * scalars + [VMEM] * (len(operands) - scalars)),
        out_specs=tuple(puts or [VMEM] * len(outs)),
        scratch_shapes=list(scratch),
        compiler_params=pltpu.CompilerParams(vmem_limit_bytes=grant * 1024 * 1024),
        cost_estimate=pl.CostEstimate(flops=flops, bytes_accessed=moved, transcendentals=0),
        name=name,
    )(*behind, *operands)


def per_device(flight_fields, top_fields, slowness, ref_slowness, flight_blocks, top_block):
    slabs, chips = lax.axis_size("depth"), lax.axis_size("z")
    own, length_y = flight_fields.shape[3:]
    rows = 2 * own
    length_x = rows * chips
    half = length_y // 2
    block = half // chips
    cells = own * length_y
    tables_x = cas_tables(length_x)
    even_y, even_y_t, odd_y, odd_y_t = tables_x if length_x == length_y else cas_tables(length_y)

    def of(shape, dtype=BF16):
        return jax.ShapeDtypeStruct(shape, dtype)

    def other_core(value):
        return lax.ppermute(value, "core", [(0, 1), (1, 0)])

    fields = flight_fields.reshape(2 * rows, length_y)
    top = top_fields.reshape(2 * rows, length_y)
    mine = slowness[0]
    fields_other, top_other, other = other_core(fields), other_core(top), other_core(mine)
    def factors(stage, odd, behind):
        return call(
            functools.partial(factors_kernel, odd, length_y, stage), (settings,),
            [of((length_x, block), F32)] * 2, flops=400 * cells, name="factors", scalars=1,
            behind=behind,
        )

    def phases(stage, behind):
        return call(
            functools.partial(phase_kernel, stage), (settings, mine, other),
            [of((rows, length_y), F32)] * 2, flops=800 * cells, name="phases", scalars=1,
            behind=behind,
        )

    pieces_of = [of((rows, 2 * block))] * chips
    lines = (2 * rows, half)
    part = pltpu.VMEM(lines, BF16)
    flops = 2 * 2 * rows * half * half
    x_part = pltpu.VMEM((length_x, 2 * block), BF16)

    def exchange(pieces, down=0):
        got = []
        for k, piece in zip(partners(chips), pieces):
            if down:
                pairs = [
                    (d * chips + z, (d + down) % slabs * chips + (z ^ k))
                    for d in range(slabs)
                    for z in range(chips)
                ]
                got.append(lax.ppermute(piece, ("depth", "z"), pairs))
            else:
                pairs = [(z, z ^ k) for z in range(chips)]
                got.append(lax.ppermute(piece, "z", pairs) if k else piece)
        return got

    def along_x(pieces, factor, behind=()):
        return call(
            functools.partial(along_x_kernel, chips), (*factor, *tables_x, *pieces),
            pieces_of, [x_part, x_part], 2 * flops, "along_x", behind=behind,
        )

    def even_part(pieces):
        return call(
            even_part_kernel, (even_y, *pieces), [of(lines, F32)], [part], flops, "even_part"
        )[0]

    share = (rows, half)
    own_evens, own_odds = call(
        own_modes_kernel, (fields, even_y_t, odd_y_t), [of(share)] * 2,
        [
            pltpu.VMEM((rows, length_y), BF16), pltpu.VMEM((2, half, half), BF16),
            pltpu.SemaphoreType.DMA((3,)),
        ],
        flops, "own_modes", ins=[HBM] * 3, grant=58,
    )
    evens = call(
        functools.partial(to_modes_kernel, 0), (fields_other, own_evens, even_y_t),
        pieces_of, [pltpu.VMEM(share, BF16)], flops // 2, "even_to_modes",
    )
    *odds, settings = call(
        odd_to_modes_kernel,
        (flight_blocks, top_block, ref_slowness, fields_other, own_odds, odd_y_t),
        pieces_of + [of((4,), F32)], [pltpu.VMEM(share, BF16)], flops // 2, "odd_to_modes",
        scalars=3, behind=(top_other, other), puts=[VMEM] * chips + [SMEM],
    )
    even_factors, odd_factors = factors(0, 0, ()), factors(0, 1, ())
    first_phases = phases(0, ())
    evens, odds = exchange(evens), exchange(odds)
    evens = exchange(along_x(evens, even_factors, (odd_factors[0], first_phases[0])))
    odds = exchange(along_x(odds, odd_factors))
    *evens, folded, first = call(
        functools.partial(turn_around_kernel, chips),
        (*first_phases, top, top_other, even_y_t, odd_y, even_part(evens), *odds),
        pieces_of + [of(lines), of((2 * rows, length_y))], [part, part], 2 * flops, "turn_around",
    )
    odds = call(odd_modes_kernel, (folded, odd_y_t), pieces_of, [part], flops, "odd_modes")
    ready = (odds[-1],)
    even_factors, odd_factors = factors(1, 0, ready), factors(1, 1, ready)
    second_phases = phases(1, ready)
    evens, odds = exchange(evens, 1), exchange(odds, 1)
    evens = exchange(along_x(evens, even_factors, (odd_factors[0], second_phases[0])))
    odds = along_x(odds, odd_factors)
    first_other = other_core(
        call(other_rows_kernel, (first,), [of((rows, length_y))], name="other_rows", behind=odds[-1:])[0]
    )
    odds = exchange(odds)
    first_part = even_part(evens)
    give, keep = [
        call(
            functools.partial(half_space_kernel, index),
            (*second_phases, odd_y, first_part, *odds),
            [of((rows, length_y))], [pltpu.VMEM((rows, half), BF16)], flops // 2, "half_space",
        )[0]
        for index in (1, 0)
    ]
    got = other_core(give)
    fields, image = call(
        finish_kernel, (first, first_other, keep, got),
        [of((2 * rows, length_y)), of((own, length_y), F32)], flops=8 * cells, name="finish",
    )
    return image[None], fields.reshape(flight_fields.shape)


def passed_along(value, axis, steps):
    count = lax.axis_size(axis)
    leading, last = (max(0, -steps), min(count, count - steps))
    return lax.ppermute(value, axis, [(source, source + steps) for source in range(leading, last)])


def make_table(length):
    positions = jnp.arange(length, dtype=jnp.int32)
    product = positions[:, None] * positions[None, :] % length
    angles = product.astype(jnp.float32) * (2.0 * math.pi / length)
    scaling = 1.0 / math.sqrt(length)
    return (jnp.concatenate([jnp.cos(angles), jnp.sin(angles)], axis=1) * scaling).astype(
        jnp.bfloat16
    )


def wavenumber(positions, length):
    signed = jnp.where(positions < length // 2, positions, positions - length)
    return signed.astype(jnp.float32) * (2.0 * math.pi / length)


def mix(product, along, half_size, orient):
    cosine_part = lax.slice_in_dim(product, 0, half_size, axis=along)
    sine_part = lax.slice_in_dim(product, half_size, 2 * half_size, axis=along)
    real_part = cosine_part[:, 0] + orient * sine_part[:, 1]
    imag_part = cosine_part[:, 1] - orient * sine_part[:, 0]
    return jnp.stack([real_part, imag_part], axis=1)


def rotate(values, cosines, sine_vals):
    real_part = values[:, 0] * cosines - values[:, 1] * sine_vals
    imag_part = values[:, 0] * sine_vals + values[:, 1] * cosines
    return jnp.stack([real_part, imag_part], axis=1)


def spectral(angular, reference_s, wave_x, wave_y):
    quad = (angular * reference_s) ** 2 - wave_x * wave_x - wave_y * wave_y
    travel = jnp.sqrt(jnp.maximum(quad, 0.0)) * step_length
    damping = jnp.exp(-jnp.sqrt(jnp.maximum(-quad, 0.0)) * step_length)
    cosines = damping * jnp.cos(travel)
    sine_vals = damping * jnp.sin(travel)
    return (jnp.stack([cosines, cosines]), jnp.stack([sine_vals, -sine_vals]))


def propagate(fields, spec_cos, spec_sin, space_cos, space_sin, to_cols, to_rows, table_x, table_y):
    length_y = table_y.shape[0]
    length_x = table_x.shape[0]
    product = jnp.einsum("fcry,yk->fckr", fields, table_y, preferred_element_type=jnp.float32)
    first = mix(product, 2, length_y, 1.0).astype(jnp.bfloat16)
    columns = to_cols(first)
    product = jnp.dot(columns, table_x, preferred_element_type=jnp.float32)
    spectrum = mix(product, 3, length_x, 1.0)
    shifted = rotate(spectrum, spec_cos, spec_sin).astype(jnp.bfloat16)
    product = jnp.dot(shifted, table_x, preferred_element_type=jnp.float32)
    back_x = mix(product, 3, length_x, -1.0).astype(jnp.bfloat16)
    rows_back = to_rows(back_x)
    product = jnp.einsum("fckr,ky->fcry", rows_back, table_y, preferred_element_type=jnp.float32)
    space = mix(product, 3, length_y, -1.0)
    return rotate(space, space_cos, space_sin).astype(jnp.bfloat16)


def together_cols(values):
    return lax.all_to_all(values, "trans", split_axis=2, concat_axis=3, tiled=True)


def together_rows(values):
    return lax.all_to_all(values, "trans", split_axis=3, concat_axis=2, tiled=True)


def advance(fields, block_id, slowness, ref_slowness, table_x, table_y):
    length_x = table_x.shape[0]
    length_y = table_y.shape[0]
    trans_count = lax.axis_size("trans")
    local_ky = length_y // trans_count
    ky_rows = lax.axis_index("trans") * local_ky + jnp.arange(local_ky, dtype=jnp.int32)
    wave_y = wavenumber(ky_rows, length_y)[:, None]
    wave_x = wavenumber(jnp.arange(length_x, dtype=jnp.int32), length_x)[None, :]
    angular = omega_top * (block_id.astype(jnp.float32) + 1.0) / NFREQ
    reference_s = ref_slowness[0]
    spec_cos, spec_sin = spectral(angular, reference_s, wave_x, wave_y)
    rotation = angular * (slowness[0] - reference_s) * step_length
    cos_r = jnp.cos(rotation)
    sin_r = jnp.sin(rotation)
    space_cos = jnp.stack([cos_r, cos_r])
    space_sin = jnp.stack([sin_r, -sin_r])
    fields = propagate(
        fields,
        spec_cos,
        spec_sin,
        space_cos,
        space_sin,
        together_cols,
        together_rows,
        table_x,
        table_y,
    )
    values = fields.astype(jnp.float32)
    terms = [values[0, 0] * values[1, 0] + values[0, 1] * values[1, 1]]
    return (fields, jnp.stack(terms))


def general_per_device(flight_fields, top_fields, slowness, ref_slowness, flight_blocks, top_block):
    table_x = make_table(flight_fields.shape[3] * lax.axis_size("trans"))
    table_y = make_table(flight_fields.shape[4])
    depth_idx = lax.axis_index("depth")
    first_block = flight_blocks[depth_idx]
    above_block = flight_blocks[jnp.maximum(depth_idx - 1, 0)]
    second_block = jnp.where(depth_idx == 0, top_block[0], above_block)
    after_first, first_terms = advance(
        flight_fields[0], first_block, slowness, ref_slowness, table_x, table_y
    )
    handed = passed_along(after_first, "depth", 1)
    incoming = jnp.where(depth_idx == 0, top_fields, handed)
    after_second, second_terms = advance(
        incoming, second_block, slowness, ref_slowness, table_x, table_y
    )
    return (first_terms + second_terms, after_second[None])


def solution(mesh):
    slabs, count = mesh.shape["depth"], mesh.shape["trans"]
    chips = count // 2

    def mapped(body, over, trans):
        placed = (
            P("depth", None, None, trans, None),
            P(None, None, trans, None),
            P("depth", trans, None),
            P("depth"),
            P(),
            P(),
        )
        return jax.shard_map(
            body,
            mesh=over,
            in_specs=placed,
            out_specs=(P("depth", trans, None), P("depth", None, None, trans, None)),
            check_vma=False,
        )

    def run(*arrays):
        length_x, length_y = arrays[0].shape[3:]
        fits = count % 2 == 0 and chips & (chips - 1) == 0
        fits = fits and length_y % (256 * chips) == 0 and length_y % 512 == 0
        if not fits or length_x % (32 * chips) or length_x % 128:
            return mapped(general_per_device, mesh, "trans")(*arrays)
        cores = Mesh(mesh.devices.reshape(slabs, chips, 2), ("depth", "z", "core"))
        return mapped(per_device, cores, ("z", "core"))(*arrays)

    return run
```

```python
import functools
import math

import jax
import jax.numpy as jnp
import numpy as np
from jax import lax
from jax.experimental import pallas as pl
from jax.experimental.pallas import tpu as pltpu
from jax.sharding import Mesh, PartitionSpec as P

NFREQ = 256

omega_top = 4.0
step_length = 0.5

VMEM = pl.BlockSpec(memory_space=pltpu.VMEM)
SMEM = pl.BlockSpec(memory_space=pltpu.SMEM)
ANY = pl.BlockSpec(memory_space=pl.ANY)
HBM = pl.BlockSpec(memory_space=pltpu.HBM)
F32 = jnp.float32
BF16 = jnp.bfloat16


def partners(count):
    return sorted(range(count), key=lambda k: (-k.bit_length(), k))


def cas_tables(length):
    positions = np.arange(length // 2, dtype=np.int64)
    quarter = length // 4

    def table(low):
        modes = np.concatenate([low, np.where(low == 0, length // 2, -low)])
        angles = (modes[:, None] * positions[None, :] % length) * (2.0 * math.pi / length)
        return ((np.cos(angles) + np.sin(angles)) / math.sqrt(length)).astype(jnp.bfloat16)

    both = [table(2 * positions[:quarter] + odd) for odd in (0, 1)]
    return [jnp.asarray(t) for one in both for t in (one, one.T.copy())]


def wave(index, length, odd):
    quarter = length // 4
    low = jnp.where(index < quarter, index, index - quarter)
    mode = 2 * low + odd
    if not odd:
        mode = jnp.where(index == quarter, length // 2, mode)
    return mode.astype(F32) * (2.0 * math.pi / length)


def dot(left, right):
    return jnp.dot(left, right, preferred_element_type=F32)


def fitted(function, degree):
    nodes = 2.1 * (1.0 + np.cos(math.pi * (np.arange(64) + 0.5) / 64))
    fit = np.polynomial.Chebyshev.fit(nodes, function(np.sqrt(nodes)), degree, domain=[0, 4.2])
    return [float(c) for c in fit.convert(kind=np.polynomial.Polynomial).coef]


COSINE = fitted(np.cos, 5)
SINE = fitted(lambda angle: np.sin(angle) / angle, 5)


def field_sign():
    return jnp.where(lax.axis_index("core") == 1, -1.0, 1.0)


def cos_sin(angle):
    square = angle * angle
    cosine = jnp.full_like(square, COSINE[-1])
    for coefficient in COSINE[-2::-1]:
        cosine = cosine * square + coefficient
    sine = jnp.full_like(square, SINE[-1])
    for coefficient in SINE[-2::-1]:
        sine = sine * square + coefficient
    return cosine, sine * angle


def factors_kernel(odd, length_y, stage, settings_ref, cos_ref, sin_ref):
    length_x, modes = cos_ref.shape
    quarter = length_x // 4
    angular, reference_s = settings_ref[2 * stage], settings_ref[2 * stage + 1]
    sign = field_sign()
    step = min(64, quarter)
    lane = lax.broadcasted_iota(jnp.int32, (step, modes), 1)
    line = lax.broadcasted_iota(jnp.int32, (step, modes), 0)
    wave_y = wave(lax.axis_index("z") * modes + lane, length_y, odd)
    constant = (angular * reference_s) ** 2 - wave_y * wave_y

    def work_out(wave_x, constant):
        quad = constant - wave_x * wave_x
        root = jnp.sqrt(jnp.abs(quad)) * step_length
        travels = quad > 0.0
        cosine, sine = cos_sin(jnp.where(travels, root, 0.0))
        damping = jnp.exp(jnp.where(travels, 0.0, -root))
        return damping * cosine, (sign * damping) * sine

    for x_odd in range(2):
        for start in range(0, quarter, step):
            values = work_out(wave(start + line, length_x, x_odd), constant)
            for half in range(2):
                at = (2 * x_odd + half) * quarter + start
                cos_ref[at : at + step, :], sin_ref[at : at + step, :] = values
    values = work_out(wave(quarter + line[:8], length_x, 0), constant[:8])
    cos_ref[quarter : quarter + 8, :], sin_ref[quarter : quarter + 8, :] = values


def phase_kernel(stage, settings_ref, mine_ref, other_ref, cos_ref, sin_ref):
    angular, reference_s = settings_ref[2 * stage], settings_ref[2 * stage + 1]
    sign = field_sign()
    rows = mine_ref.shape[0]
    step = 8
    for index, slowness in enumerate((mine_ref, other_ref)):
        start = (lax.axis_index("core") ^ index) * rows

        @pl.loop(0, rows // step)
        def _(chunk):
            there = pl.ds(pl.multiple_of(start + chunk * step, step), step)
            here = pl.ds(pl.multiple_of(chunk * step, step), step)
            cosine, sine = cos_sin(angular * (slowness[here, :] - reference_s) * step_length)
            cos_ref[there, :] = cosine
            sin_ref[there, :] = sign * sine


def rows_of(start, size):
    return pl.ds(pl.multiple_of(start, size), size)


def split_modes(here, whole, outs):
    rows, width = outs[0].shape
    block = width // 2
    for k, out in zip(partners(len(outs)), outs):
        columns = rows_of((here ^ k) * block, block)
        for part in range(2):
            out[:, part * block : (part + 1) * block] = whole[
                part * rows : (part + 1) * rows, columns
            ]


def join_modes(here, pieces, whole, lines=None):
    rows, width = pieces[0].shape
    block = width // 2
    size = rows if lines is None else lines.size
    for k, piece in zip(partners(len(pieces)), pieces):
        columns = rows_of((here ^ k) * block, block)
        for part in range(2):
            whole[part * size : (part + 1) * size, columns] = piece[
                slice(None) if lines is None else lines, part * block : (part + 1) * block
            ]


def own_modes_kernel(fields_ref, table_ref, out_ref):
    rows, half = out_ref.shape
    mine = rows_of(lax.axis_index("core") * rows, rows)
    out_ref[...] = dot(fields_ref[mine, :half] + fields_ref[mine, half:], table_ref[...]).astype(BF16)


def even_to_modes_kernel(other_ref, own_ref, table_ref, *refs):
    outs, modes = refs[:-1], refs[-1]
    rows, half = own_ref.shape
    own = rows // 2
    core = lax.axis_index("core")
    theirs = rows_of(core * rows, rows)
    modes[...] = dot(other_ref[theirs, :half] + other_ref[theirs, half:], table_ref[...]).astype(BF16)
    block = half // len(outs)
    for k, out in zip(partners(len(outs)), outs):
        columns = rows_of((lax.axis_index("z") ^ k) * block, block)
        for part in range(2):
            lanes = slice(part * block, (part + 1) * block)
            lines = slice(part * own, (part + 1) * own)
            out[rows_of(core * own, own), lanes] = own_ref[lines, columns]
            out[rows_of((core ^ 1) * own, own), lanes] = modes[lines, columns]


def odd_pieces(fields_ref, other_ref, table_ref, *refs):
    outs, (folded, modes) = refs[:-2], refs[-2:]
    half = table_ref.shape[0]
    own = folded.shape[0] // 4
    core = lax.axis_index("core")
    for part in range(2):
        mine = rows_of((2 * core + part) * own, own)
        for index, source in enumerate((fields_ref, other_ref)):
            there = rows_of(2 * part * own + (core ^ index) * own, own)
            folded[there, :] = source[mine, :half] - source[mine, half:]
    modes[...] = dot(folded[...], table_ref[...]).astype(BF16)
    split_modes(lax.axis_index("z"), modes, outs)


def odd_to_modes_kernel(blocks_ref, top_block_ref, reference_ref, *refs):
    settings_ref = refs[-3]
    depth = lax.axis_index("depth")
    above = blocks_ref[jnp.maximum(depth - 1, 0)]
    second = jnp.where(depth == 0, top_block_ref[0], above)
    for index, block in enumerate((blocks_ref[depth], second)):
        settings_ref[2 * index] = omega_top * (block.astype(F32) + 1.0) / NFREQ
        settings_ref[2 * index + 1] = reference_ref[0]
    odd_pieces(*refs[:-3], *refs[-2:])


def along_x_kernel(
    count, cos_ref, sin_ref, even_ref, even_t_ref, odd_ref, odd_t_ref, *refs
):
    pieces, outs = refs[:count], refs[count : 2 * count]
    held, shifted = refs[2 * count :]
    here = lax.axis_index("z")
    rows, width = outs[0].shape
    block = width // 2
    for k, piece in zip(partners(count), pieces):
        held[rows_of((here ^ k) * rows, rows), :] = piece[...]
    half = even_ref.shape[0]
    low, high = held[:half, :], held[half:, :]
    for part, table, values in ((0, even_ref, low + high), (1, odd_ref, low - high)):
        lines = slice(part * half, (part + 1) * half)
        spectrum = dot(table[...], values)
        real, imag = spectrum[:, :block], spectrum[:, block:]
        cosine, sine = cos_ref[lines, :], sin_ref[lines, :]
        shifted[lines, :block] = (real * cosine - imag * sine).astype(BF16)
        shifted[lines, block:] = (real * sine + imag * cosine).astype(BF16)
    first = dot(even_t_ref[...], shifted[:half, :])
    second = dot(odd_t_ref[...], shifted[half:, :])
    held[:half, :] = (first + second).astype(BF16)
    held[half:, :] = (first - second).astype(BF16)
    for k, out in zip(partners(count), outs):
        out[...] = held[rows_of((here ^ k) * rows, rows), :]


def even_part_kernel(table_ref, *refs):
    pieces, (out_ref, modes) = refs[:-2], refs[-2:]
    join_modes(lax.axis_index("z"), pieces, modes)
    out_ref[...] = dot(modes[...], table_ref[...])


def turned(real, imag, cosine, sine):
    return (real * cosine - imag * sine).astype(BF16), (real * sine + imag * cosine).astype(BF16)


def turn_around_kernel(
    count, cos_ref, sin_ref, top_ref, top_other_ref, even_t_ref, odd_ref, part_ref, *refs
):
    pieces, outs = refs[:count], refs[count : 2 * count]
    folded_ref, both_ref, modes, sums = refs[2 * count :]
    here, core = lax.axis_index("z"), lax.axis_index("core")
    rows = pieces[0].shape[0]
    own = rows // 2
    half = odd_ref.shape[0]
    join_modes(here, pieces, modes)
    step = 256
    for start in range(0, half, step):
        columns = slice(start, start + step)
        second = dot(modes[...], odd_ref[:, columns])
        first = part_ref[:, columns]
        stepped = []
        for values, at in ((first + second, start), (first - second, start + half)):
            lanes = slice(at, at + step)
            fields = turned(values[:rows], values[rows:], cos_ref[:, lanes], sin_ref[:, lanes])
            stepped.append(fields)
            for index in range(2):
                for part, field in enumerate(fields):
                    there = (2 * index + part) * own
                    both_ref[there : there + own, lanes] = field[index * own : (index + 1) * own]
        for part in range(2):
            lines = slice(part * rows, (part + 1) * rows)
            sums[lines, columns] = stepped[0][part] + stepped[1][part]
            folded_ref[lines, columns] = stepped[0][part] - stepped[1][part]

    @pl.when(lax.axis_index("depth") == lax.axis_size("depth") - 1)
    def _():
        for index, source in enumerate((top_ref, top_other_ref)):
            for part in range(2):
                lines = rows_of((2 * core + part) * own, own)
                low, high = source[lines, :half], source[lines, half:]
                there = rows_of(part * rows + (core ^ index) * own, own)
                sums[there, :] = low + high
                folded_ref[there, :] = low - high

    modes[...] = dot(sums[...], even_t_ref[...]).astype(BF16)
    split_modes(here, modes, outs)


def odd_modes_kernel(folded_ref, table_ref, *refs):
    outs, modes = refs[:-1], refs[-1]
    modes[...] = dot(folded_ref[...], table_ref[...]).astype(BF16)
    split_modes(lax.axis_index("z"), modes, outs)


def half_space_kernel(index, cos_ref, sin_ref, odd_ref, part_ref, *refs):
    pieces, (out_ref, modes) = refs[:-2], refs[-2:]
    rows = pieces[0].shape[0]
    own = rows // 2
    half = odd_ref.shape[0]
    offset = (lax.axis_index("core") ^ index) * own
    lines = rows_of(offset, own)
    join_modes(lax.axis_index("z"), pieces, modes, lines)
    step = 256
    for start in range(0, half, step):
        columns = slice(start, start + step)
        second = dot(modes[...], odd_ref[:, columns])
        for sign, at in ((1.0, start), (-1.0, start + half)):
            lanes = slice(at, at + step)
            real, imag = [
                part_ref[rows_of(part * rows + offset, own), columns]
                + sign * second[part * own : (part + 1) * own]
                for part in range(2)
            ]
            out_ref[:own, lanes], out_ref[own:, lanes] = turned(
                real, imag, cos_ref[lines, lanes], sin_ref[lines, lanes]
            )


def other_rows_kernel(both_ref, out_ref):
    rows = out_ref.shape[0]
    out_ref[...] = both_ref[rows_of((lax.axis_index("core") ^ 1) * rows, rows), :]


def finish_kernel(first_ref, first_other_ref, keep_ref, got_ref, fields_ref, image_ref):
    rows = keep_ref.shape[0]
    own = rows // 2
    core = lax.axis_index("core")
    fields_ref[rows_of(core * rows, rows), :] = keep_ref[...]
    fields_ref[rows_of((core ^ 1) * rows, rows), :] = got_ref[...]
    step = 16
    for start in range(0, own, step):
        total = None
        for part in range(2):
            lines = slice(part * own + start, part * own + start + step)
            mine = rows_of(core * rows + part * own + start, step)
            for one, two in (
                (first_ref[mine, :], first_other_ref[lines, :]),
                (keep_ref[lines, :], got_ref[lines, :]),
            ):
                term = one.astype(F32) * two.astype(F32)
                total = term if total is None else total + term
        image_ref[start : start + step, :] = total


def after(count, kernel, *refs):
    return kernel(*refs[count:])


def call(
    kernel, operands, outs, scratch=(), flops=0, name=None, scalars=0, behind=(), ins=None, puts=None,
    grant=24,
):
    moved = sum(math.prod(a.shape) * a.dtype.itemsize for a in operands)
    moved += sum(math.prod(a.shape) * a.dtype.itemsize for a in outs)
    return pl.pallas_call(
        functools.partial(after, len(behind), kernel),
        out_shape=tuple(outs),
        in_specs=[ANY] * len(behind)
        + (ins or [SMEM] * scalars + [VMEM] * (len(operands) - scalars)),
        out_specs=tuple(puts or [VMEM] * len(outs)),
        scratch_shapes=list(scratch),
        compiler_params=pltpu.CompilerParams(vmem_limit_bytes=grant * 1024 * 1024),
        cost_estimate=pl.CostEstimate(flops=flops, bytes_accessed=moved, transcendentals=0),
        name=name,
    )(*behind, *operands)


def per_device(flight_fields, top_fields, slowness, ref_slowness, flight_blocks, top_block):
    slabs, chips = lax.axis_size("depth"), lax.axis_size("z")
    own, length_y = flight_fields.shape[3:]
    rows = 2 * own
    length_x = rows * chips
    half = length_y // 2
    block = half // chips
    cells = own * length_y
    tables_x = cas_tables(length_x)
    even_y, even_y_t, odd_y, odd_y_t = tables_x if length_x == length_y else cas_tables(length_y)

    def of(shape, dtype=BF16):
        return jax.ShapeDtypeStruct(shape, dtype)

    def other_core(value):
        return lax.ppermute(value, "core", [(0, 1), (1, 0)])

    fields = flight_fields.reshape(2 * rows, length_y)
    top = top_fields.reshape(2 * rows, length_y)
    mine = slowness[0]
    fields_other, top_other, other = other_core(fields), other_core(top), other_core(mine)
    def factors(stage, odd, behind):
        return call(
            functools.partial(factors_kernel, odd, length_y, stage), (settings,),
            [of((length_x, block), F32)] * 2, flops=400 * cells, name="factors", scalars=1,
            behind=behind,
        )

    def phases(stage, behind):
        return call(
            functools.partial(phase_kernel, stage), (settings, mine, other),
            [of((rows, length_y), F32)] * 2, flops=800 * cells, name="phases", scalars=1,
            behind=behind,
        )

    pieces_of = [of((rows, 2 * block))] * chips
    lines = (2 * rows, half)
    part = pltpu.VMEM(lines, BF16)
    flops = 2 * 2 * rows * half * half
    x_part = pltpu.VMEM((length_x, 2 * block), BF16)

    def exchange(pieces, down=0):
        got = []
        for k, piece in zip(partners(chips), pieces):
            if down:
                pairs = [
                    (d * chips + z, (d + down) % slabs * chips + (z ^ k))
                    for d in range(slabs)
                    for z in range(chips)
                ]
                got.append(lax.ppermute(piece, ("depth", "z"), pairs))
            else:
                pairs = [(z, z ^ k) for z in range(chips)]
                got.append(lax.ppermute(piece, "z", pairs) if k else piece)
        return got

    def along_x(pieces, factor, behind=()):
        return call(
            functools.partial(along_x_kernel, chips), (*factor, *tables_x, *pieces),
            pieces_of, [x_part, x_part], 2 * flops, "along_x", behind=behind,
        )

    def even_part(pieces):
        return call(
            even_part_kernel, (even_y, *pieces), [of(lines, F32)], [part], flops, "even_part"
        )[0]

    share = (rows, half)
    own_evens = call(
        own_modes_kernel, (fields, even_y_t), [of(share)], flops=flops // 2, name="own_modes"
    )[0]
    evens = call(
        even_to_modes_kernel, (fields_other, own_evens, even_y_t),
        pieces_of, [pltpu.VMEM(share, BF16)], flops // 2, "even_to_modes",
    )
    *odds, settings = call(
        odd_to_modes_kernel,
        (flight_blocks, top_block, ref_slowness, fields, fields_other, odd_y_t),
        pieces_of + [of((4,), F32)], [part, part], flops, "odd_to_modes",
        scalars=3, behind=(top_other, other), puts=[VMEM] * chips + [SMEM],
    )
    even_factors, odd_factors = factors(0, 0, ()), factors(0, 1, ())
    first_phases = phases(0, ())
    evens, odds = exchange(evens), exchange(odds)
    evens = exchange(along_x(evens, even_factors, (odd_factors[0], first_phases[0])))
    odds = exchange(along_x(odds, odd_factors))
    *evens, folded, first = call(
        functools.partial(turn_around_kernel, chips),
        (*first_phases, top, top_other, even_y_t, odd_y, even_part(evens), *odds),
        pieces_of + [of(lines), of((2 * rows, length_y))], [part, part], 2 * flops, "turn_around",
    )
    odds = call(odd_modes_kernel, (folded, odd_y_t), pieces_of, [part], flops, "odd_modes")
    ready = (odds[-1],)
    even_factors, odd_factors = factors(1, 0, ready), factors(1, 1, ready)
    second_phases = phases(1, ready)
    evens, odds = exchange(evens, 1), exchange(odds, 1)
    evens = exchange(along_x(evens, even_factors, (odd_factors[0], second_phases[0])))
    odds = along_x(odds, odd_factors)
    first_other = other_core(
        call(other_rows_kernel, (first,), [of((rows, length_y))], name="other_rows", behind=odds[-1:])[0]
    )
    odds = exchange(odds)
    first_part = even_part(evens)
    give, keep = [
        call(
            functools.partial(half_space_kernel, index),
            (*second_phases, odd_y, first_part, *odds),
            [of((rows, length_y))], [pltpu.VMEM((rows, half), BF16)], flops // 2, "half_space",
        )[0]
        for index in (1, 0)
    ]
    got = other_core(give)
    fields, image = call(
        finish_kernel, (first, first_other, keep, got),
        [of((2 * rows, length_y)), of((own, length_y), F32)], flops=8 * cells, name="finish",
    )
    return image[None], fields.reshape(flight_fields.shape)


def passed_along(value, axis, steps):
    count = lax.axis_size(axis)
    leading, last = (max(0, -steps), min(count, count - steps))
    return lax.ppermute(value, axis, [(source, source + steps) for source in range(leading, last)])


def make_table(length):
    positions = jnp.arange(length, dtype=jnp.int32)
    product = positions[:, None] * positions[None, :] % length
    angles = product.astype(jnp.float32) * (2.0 * math.pi / length)
    scaling = 1.0 / math.sqrt(length)
    return (jnp.concatenate([jnp.cos(angles), jnp.sin(angles)], axis=1) * scaling).astype(
        jnp.bfloat16
    )


def wavenumber(positions, length):
    signed = jnp.where(positions < length // 2, positions, positions - length)
    return signed.astype(jnp.float32) * (2.0 * math.pi / length)


def mix(product, along, half_size, orient):
    cosine_part = lax.slice_in_dim(product, 0, half_size, axis=along)
    sine_part = lax.slice_in_dim(product, half_size, 2 * half_size, axis=along)
    real_part = cosine_part[:, 0] + orient * sine_part[:, 1]
    imag_part = cosine_part[:, 1] - orient * sine_part[:, 0]
    return jnp.stack([real_part, imag_part], axis=1)


def rotate(values, cosines, sine_vals):
    real_part = values[:, 0] * cosines - values[:, 1] * sine_vals
    imag_part = values[:, 0] * sine_vals + values[:, 1] * cosines
    return jnp.stack([real_part, imag_part], axis=1)


def spectral(angular, reference_s, wave_x, wave_y):
    quad = (angular * reference_s) ** 2 - wave_x * wave_x - wave_y * wave_y
    travel = jnp.sqrt(jnp.maximum(quad, 0.0)) * step_length
    damping = jnp.exp(-jnp.sqrt(jnp.maximum(-quad, 0.0)) * step_length)
    cosines = damping * jnp.cos(travel)
    sine_vals = damping * jnp.sin(travel)
    return (jnp.stack([cosines, cosines]), jnp.stack([sine_vals, -sine_vals]))


def propagate(fields, spec_cos, spec_sin, space_cos, space_sin, to_cols, to_rows, table_x, table_y):
    length_y = table_y.shape[0]
    length_x = table_x.shape[0]
    product = jnp.einsum("fcry,yk->fckr", fields, table_y, preferred_element_type=jnp.float32)
    first = mix(product, 2, length_y, 1.0).astype(jnp.bfloat16)
    columns = to_cols(first)
    product = jnp.dot(columns, table_x, preferred_element_type=jnp.float32)
    spectrum = mix(product, 3, length_x, 1.0)
    shifted = rotate(spectrum, spec_cos, spec_sin).astype(jnp.bfloat16)
    product = jnp.dot(shifted, table_x, preferred_element_type=jnp.float32)
    back_x = mix(product, 3, length_x, -1.0).astype(jnp.bfloat16)
    rows_back = to_rows(back_x)
    product = jnp.einsum("fckr,ky->fcry", rows_back, table_y, preferred_element_type=jnp.float32)
    space = mix(product, 3, length_y, -1.0)
    return rotate(space, space_cos, space_sin).astype(jnp.bfloat16)


def together_cols(values):
    return lax.all_to_all(values, "trans", split_axis=2, concat_axis=3, tiled=True)


def together_rows(values):
    return lax.all_to_all(values, "trans", split_axis=3, concat_axis=2, tiled=True)


def advance(fields, block_id, slowness, ref_slowness, table_x, table_y):
    length_x = table_x.shape[0]
    length_y = table_y.shape[0]
    trans_count = lax.axis_size("trans")
    local_ky = length_y // trans_count
    ky_rows = lax.axis_index("trans") * local_ky + jnp.arange(local_ky, dtype=jnp.int32)
    wave_y = wavenumber(ky_rows, length_y)[:, None]
    wave_x = wavenumber(jnp.arange(length_x, dtype=jnp.int32), length_x)[None, :]
    angular = omega_top * (block_id.astype(jnp.float32) + 1.0) / NFREQ
    reference_s = ref_slowness[0]
    spec_cos, spec_sin = spectral(angular, reference_s, wave_x, wave_y)
    rotation = angular * (slowness[0] - reference_s) * step_length
    cos_r = jnp.cos(rotation)
    sin_r = jnp.sin(rotation)
    space_cos = jnp.stack([cos_r, cos_r])
    space_sin = jnp.stack([sin_r, -sin_r])
    fields = propagate(
        fields,
        spec_cos,
        spec_sin,
        space_cos,
        space_sin,
        together_cols,
        together_rows,
        table_x,
        table_y,
    )
    values = fields.astype(jnp.float32)
    terms = [values[0, 0] * values[1, 0] + values[0, 1] * values[1, 1]]
    return (fields, jnp.stack(terms))


def general_per_device(flight_fields, top_fields, slowness, ref_slowness, flight_blocks, top_block):
    table_x = make_table(flight_fields.shape[3] * lax.axis_size("trans"))
    table_y = make_table(flight_fields.shape[4])
    depth_idx = lax.axis_index("depth")
    first_block = flight_blocks[depth_idx]
    above_block = flight_blocks[jnp.maximum(depth_idx - 1, 0)]
    second_block = jnp.where(depth_idx == 0, top_block[0], above_block)
    after_first, first_terms = advance(
        flight_fields[0], first_block, slowness, ref_slowness, table_x, table_y
    )
    handed = passed_along(after_first, "depth", 1)
    incoming = jnp.where(depth_idx == 0, top_fields, handed)
    after_second, second_terms = advance(
        incoming, second_block, slowness, ref_slowness, table_x, table_y
    )
    return (first_terms + second_terms, after_second[None])


def solution(mesh):
    slabs, count = mesh.shape["depth"], mesh.shape["trans"]
    chips = count // 2

    def mapped(body, over, trans):
        placed = (
            P("depth", None, None, trans, None),
            P(None, None, trans, None),
            P("depth", trans, None),
            P("depth"),
            P(),
            P(),
        )
        return jax.shard_map(
            body,
            mesh=over,
            in_specs=placed,
            out_specs=(P("depth", trans, None), P("depth", None, None, trans, None)),
            check_vma=False,
        )

    def run(*arrays):
        length_x, length_y = arrays[0].shape[3:]
        fits = count % 2 == 0 and chips & (chips - 1) == 0
        fits = fits and length_y % (256 * chips) == 0 and length_y % 512 == 0
        if not fits or length_x % (32 * chips) or length_x % 128:
            return mapped(general_per_device, mesh, "trans")(*arrays)
        cores = Mesh(mesh.devices.reshape(slabs, chips, 2), ("depth", "z", "core"))
        return mapped(per_device, cores, ("z", "core"))(*arrays)

    return run
```

```python
import functools
import math

import jax
import jax.numpy as jnp
import numpy as np
from jax import lax
from jax.experimental import pallas as pl
from jax.experimental.pallas import tpu as pltpu
from jax.sharding import Mesh, PartitionSpec as P

NFREQ = 256

omega_top = 4.0
step_length = 0.5

VMEM = pl.BlockSpec(memory_space=pltpu.VMEM)
SMEM = pl.BlockSpec(memory_space=pltpu.SMEM)
ANY = pl.BlockSpec(memory_space=pl.ANY)
HBM = pl.BlockSpec(memory_space=pltpu.HBM)
F32 = jnp.float32
BF16 = jnp.bfloat16


def partners(count):
    return sorted(range(count), key=lambda k: (-k.bit_length(), k))


def cas_tables(length):
    positions = np.arange(length // 2, dtype=np.int64)
    quarter = length // 4

    def table(low):
        modes = np.concatenate([low, np.where(low == 0, length // 2, -low)])
        angles = (modes[:, None] * positions[None, :] % length) * (2.0 * math.pi / length)
        return ((np.cos(angles) + np.sin(angles)) / math.sqrt(length)).astype(jnp.bfloat16)

    both = [table(2 * positions[:quarter] + odd) for odd in (0, 1)]
    return [jnp.asarray(t) for one in both for t in (one, one.T.copy())]


def wave(index, length, odd):
    quarter = length // 4
    low = jnp.where(index < quarter, index, index - quarter)
    mode = 2 * low + odd
    if not odd:
        mode = jnp.where(index == quarter, length // 2, mode)
    return mode.astype(F32) * (2.0 * math.pi / length)


def dot(left, right):
    return jnp.dot(left, right, preferred_element_type=F32)


def fitted(function, degree):
    nodes = 2.1 * (1.0 + np.cos(math.pi * (np.arange(64) + 0.5) / 64))
    fit = np.polynomial.Chebyshev.fit(nodes, function(np.sqrt(nodes)), degree, domain=[0, 4.2])
    return [float(c) for c in fit.convert(kind=np.polynomial.Polynomial).coef]


COSINE = fitted(np.cos, 5)
SINE = fitted(lambda angle: np.sin(angle) / angle, 5)


def field_sign():
    return jnp.where(lax.axis_index("core") == 1, -1.0, 1.0)


def cos_sin(angle):
    square = angle * angle
    cosine = jnp.full_like(square, COSINE[-1])
    for coefficient in COSINE[-2::-1]:
        cosine = cosine * square + coefficient
    sine = jnp.full_like(square, SINE[-1])
    for coefficient in SINE[-2::-1]:
        sine = sine * square + coefficient
    return cosine, sine * angle


def factors_kernel(odd, length_y, stage, settings_ref, cos_ref, sin_ref):
    length_x, modes = cos_ref.shape
    quarter = length_x // 4
    angular, reference_s = settings_ref[2 * stage], settings_ref[2 * stage + 1]
    sign = field_sign()
    step = min(64, quarter)
    lane = lax.broadcasted_iota(jnp.int32, (step, modes), 1)
    line = lax.broadcasted_iota(jnp.int32, (step, modes), 0)
    wave_y = wave(lax.axis_index("z") * modes + lane, length_y, odd)
    constant = (angular * reference_s) ** 2 - wave_y * wave_y

    def work_out(wave_x, constant):
        quad = constant - wave_x * wave_x
        root = jnp.sqrt(jnp.abs(quad)) * step_length
        travels = quad > 0.0
        cosine, sine = cos_sin(jnp.where(travels, root, 0.0))
        damping = jnp.exp(jnp.where(travels, 0.0, -root))
        return damping * cosine, (sign * damping) * sine

    for x_odd in range(2):
        for start in range(0, quarter, step):
            values = work_out(wave(start + line, length_x, x_odd), constant)
            for half in range(2):
                at = (2 * x_odd + half) * quarter + start
                cos_ref[at : at + step, :], sin_ref[at : at + step, :] = values
    values = work_out(wave(quarter + line[:8], length_x, 0), constant[:8])
    cos_ref[quarter : quarter + 8, :], sin_ref[quarter : quarter + 8, :] = values


def phase_kernel(stage, settings_ref, mine_ref, other_ref, cos_ref, sin_ref):
    angular, reference_s = settings_ref[2 * stage], settings_ref[2 * stage + 1]
    sign = field_sign()
    rows = mine_ref.shape[0]
    step = 8
    for index, slowness in enumerate((mine_ref, other_ref)):
        start = (lax.axis_index("core") ^ index) * rows

        @pl.loop(0, rows // step)
        def _(chunk):
            there = pl.ds(pl.multiple_of(start + chunk * step, step), step)
            here = pl.ds(pl.multiple_of(chunk * step, step), step)
            cosine, sine = cos_sin(angular * (slowness[here, :] - reference_s) * step_length)
            cos_ref[there, :] = cosine
            sin_ref[there, :] = sign * sine


def rows_of(start, size):
    return pl.ds(pl.multiple_of(start, size), size)


def split_modes(here, whole, outs):
    rows, width = outs[0].shape
    block = width // 2
    for k, out in zip(partners(len(outs)), outs):
        columns = rows_of((here ^ k) * block, block)
        for part in range(2):
            out[:, part * block : (part + 1) * block] = whole[
                part * rows : (part + 1) * rows, columns
            ]


def join_modes(here, pieces, whole, lines=None):
    rows, width = pieces[0].shape
    block = width // 2
    size = rows if lines is None else lines.size
    for k, piece in zip(partners(len(pieces)), pieces):
        columns = rows_of((here ^ k) * block, block)
        for part in range(2):
            whole[part * size : (part + 1) * size, columns] = piece[
                slice(None) if lines is None else lines, part * block : (part + 1) * block
            ]


def own_modes_kernel(fields_ref, table_ref, out_ref):
    rows, half = out_ref.shape
    mine = rows_of(lax.axis_index("core") * rows, rows)
    out_ref[...] = dot(fields_ref[mine, :half] + fields_ref[mine, half:], table_ref[...]).astype(BF16)


def even_to_modes_kernel(other_ref, own_ref, table_ref, *refs):
    outs, modes = refs[:-1], refs[-1]
    rows, half = own_ref.shape
    own = rows // 2
    core = lax.axis_index("core")
    theirs = rows_of(core * rows, rows)
    modes[...] = dot(other_ref[theirs, :half] + other_ref[theirs, half:], table_ref[...]).astype(BF16)
    block = half // len(outs)
    for k, out in zip(partners(len(outs)), outs):
        columns = rows_of((lax.axis_index("z") ^ k) * block, block)
        for part in range(2):
            lanes = slice(part * block, (part + 1) * block)
            lines = slice(part * own, (part + 1) * own)
            out[rows_of(core * own, own), lanes] = own_ref[lines, columns]
            out[rows_of((core ^ 1) * own, own), lanes] = modes[lines, columns]


def odd_pieces(fields_ref, other_ref, table_ref, *refs):
    outs, (folded, modes) = refs[:-2], refs[-2:]
    half = table_ref.shape[0]
    own = folded.shape[0] // 4
    core = lax.axis_index("core")
    for part in range(2):
        mine = rows_of((2 * core + part) * own, own)
        for index, source in enumerate((fields_ref, other_ref)):
            there = rows_of(2 * part * own + (core ^ index) * own, own)
            folded[there, :] = source[mine, :half] - source[mine, half:]
    modes[...] = dot(folded[...], table_ref[...]).astype(BF16)
    split_modes(lax.axis_index("z"), modes, outs)


def odd_to_modes_kernel(blocks_ref, top_block_ref, reference_ref, *refs):
    settings_ref = refs[-3]
    depth = lax.axis_index("depth")
    above = blocks_ref[jnp.maximum(depth - 1, 0)]
    second = jnp.where(depth == 0, top_block_ref[0], above)
    for index, block in enumerate((blocks_ref[depth], second)):
        settings_ref[2 * index] = omega_top * (block.astype(F32) + 1.0) / NFREQ
        settings_ref[2 * index + 1] = reference_ref[0]
    odd_pieces(*refs[:-3], *refs[-2:])


def along_x_kernel(
    count, cos_ref, sin_ref, even_ref, even_t_ref, odd_ref, odd_t_ref, *refs
):
    pieces, outs = refs[:count], refs[count : 2 * count]
    held, shifted = refs[2 * count :]
    here = lax.axis_index("z")
    rows, width = outs[0].shape
    block = width // 2
    for k, piece in zip(partners(count), pieces):
        held[rows_of((here ^ k) * rows, rows), :] = piece[...]
    half = even_ref.shape[0]
    low, high = held[:half, :], held[half:, :]
    for part, table, values in ((0, even_ref, low + high), (1, odd_ref, low - high)):
        lines = slice(part * half, (part + 1) * half)
        spectrum = dot(table[...], values)
        real, imag = spectrum[:, :block], spectrum[:, block:]
        cosine, sine = cos_ref[lines, :], sin_ref[lines, :]
        shifted[lines, :block] = (real * cosine - imag * sine).astype(BF16)
        shifted[lines, block:] = (real * sine + imag * cosine).astype(BF16)
    first = dot(even_t_ref[...], shifted[:half, :])
    second = dot(odd_t_ref[...], shifted[half:, :])
    held[:half, :] = (first + second).astype(BF16)
    held[half:, :] = (first - second).astype(BF16)
    for k, out in zip(partners(count), outs):
        out[...] = held[rows_of((here ^ k) * rows, rows), :]


def even_part_kernel(table_ref, *refs):
    pieces, (out_ref, modes) = refs[:-2], refs[-2:]
    join_modes(lax.axis_index("z"), pieces, modes)
    out_ref[...] = dot(modes[...], table_ref[...])


def turned(real, imag, cosine, sine):
    return (real * cosine - imag * sine).astype(BF16), (real * sine + imag * cosine).astype(BF16)


def turn_around_kernel(
    count, cos_ref, sin_ref, top_ref, top_other_ref, even_t_ref, odd_ref, part_ref, *refs
):
    pieces, outs = refs[:count], refs[count : 2 * count]
    folded_ref, both_ref, modes, sums = refs[2 * count :]
    here, core = lax.axis_index("z"), lax.axis_index("core")
    rows = pieces[0].shape[0]
    own = rows // 2
    half = odd_ref.shape[0]
    join_modes(here, pieces, modes)
    step = 512
    for start in range(0, half, step):
        columns = slice(start, start + step)
        second = dot(modes[...], odd_ref[:, columns])
        first = part_ref[:, columns]
        stepped = []
        for values, at in ((first + second, start), (first - second, start + half)):
            lanes = slice(at, at + step)
            fields = turned(values[:rows], values[rows:], cos_ref[:, lanes], sin_ref[:, lanes])
            stepped.append(fields)
            for index in range(2):
                for part, field in enumerate(fields):
                    there = (2 * index + part) * own
                    both_ref[there : there + own, lanes] = field[index * own : (index + 1) * own]
        for part in range(2):
            lines = slice(part * rows, (part + 1) * rows)
            sums[lines, columns] = stepped[0][part] + stepped[1][part]
            folded_ref[lines, columns] = stepped[0][part] - stepped[1][part]

    @pl.when(lax.axis_index("depth") == lax.axis_size("depth") - 1)
    def _():
        for index, source in enumerate((top_ref, top_other_ref)):
            for part in range(2):
                lines = rows_of((2 * core + part) * own, own)
                low, high = source[lines, :half], source[lines, half:]
                there = rows_of(part * rows + (core ^ index) * own, own)
                sums[there, :] = low + high
                folded_ref[there, :] = low - high

    modes[...] = dot(sums[...], even_t_ref[...]).astype(BF16)
    split_modes(here, modes, outs)


def odd_modes_kernel(folded_ref, table_ref, *refs):
    outs, modes = refs[:-1], refs[-1]
    modes[...] = dot(folded_ref[...], table_ref[...]).astype(BF16)
    split_modes(lax.axis_index("z"), modes, outs)


def half_space_kernel(index, cos_ref, sin_ref, odd_ref, part_ref, *refs):
    pieces, (out_ref, modes) = refs[:-2], refs[-2:]
    rows = pieces[0].shape[0]
    own = rows // 2
    half = odd_ref.shape[0]
    offset = (lax.axis_index("core") ^ index) * own
    lines = rows_of(offset, own)
    join_modes(lax.axis_index("z"), pieces, modes, lines)
    step = 512
    for start in range(0, half, step):
        columns = slice(start, start + step)
        second = dot(modes[...], odd_ref[:, columns])
        for sign, at in ((1.0, start), (-1.0, start + half)):
            lanes = slice(at, at + step)
            real, imag = [
                part_ref[rows_of(part * rows + offset, own), columns]
                + sign * second[part * own : (part + 1) * own]
                for part in range(2)
            ]
            out_ref[:own, lanes], out_ref[own:, lanes] = turned(
                real, imag, cos_ref[lines, lanes], sin_ref[lines, lanes]
            )


def other_rows_kernel(both_ref, out_ref):
    rows = out_ref.shape[0]
    out_ref[...] = both_ref[rows_of((lax.axis_index("core") ^ 1) * rows, rows), :]


def finish_kernel(
    first_ref, first_other_ref, keep_ref, got_ref, fields_out, image_out, image, sems
):
    rows = keep_ref.shape[0]
    own = rows // 2
    core = lax.axis_index("core")
    copies = [
        pltpu.make_async_copy(keep_ref, fields_out.at[rows_of(core * rows, rows), :], sems.at[0]),
        pltpu.make_async_copy(
            got_ref, fields_out.at[rows_of((core ^ 1) * rows, rows), :], sems.at[1]
        ),
    ]
    for copy in copies:
        copy.start()
    step = 16
    for start in range(0, own, step):
        total = None
        for part in range(2):
            lines = slice(part * own + start, part * own + start + step)
            mine = rows_of(core * rows + part * own + start, step)
            for one, two in (
                (first_ref[mine, :], first_other_ref[lines, :]),
                (keep_ref[lines, :], got_ref[lines, :]),
            ):
                term = one.astype(F32) * two.astype(F32)
                total = term if total is None else total + term
        image[start : start + step, :] = total
        if (start + step) % (own // 2) == 0:
            done = slice(start + step - own // 2, start + step)
            copies.append(
                pltpu.make_async_copy(
                    image.at[done, :], image_out.at[done, :], sems.at[len(copies)]
                )
            )
            copies[-1].start()
    for copy in copies:
        copy.wait()


def after(count, kernel, *refs):
    return kernel(*refs[count:])


def call(
    kernel, operands, outs, scratch=(), flops=0, name=None, scalars=0, behind=(), ins=None, puts=None,
    grant=24,
):
    moved = sum(math.prod(a.shape) * a.dtype.itemsize for a in operands)
    moved += sum(math.prod(a.shape) * a.dtype.itemsize for a in outs)
    return pl.pallas_call(
        functools.partial(after, len(behind), kernel),
        out_shape=tuple(outs),
        in_specs=[ANY] * len(behind)
        + (ins or [SMEM] * scalars + [VMEM] * (len(operands) - scalars)),
        out_specs=tuple(puts or [VMEM] * len(outs)),
        scratch_shapes=list(scratch),
        compiler_params=pltpu.CompilerParams(vmem_limit_bytes=grant * 1024 * 1024),
        cost_estimate=pl.CostEstimate(flops=flops, bytes_accessed=moved, transcendentals=0),
        name=name,
    )(*behind, *operands)


def per_device(flight_fields, top_fields, slowness, ref_slowness, flight_blocks, top_block):
    slabs, chips = lax.axis_size("depth"), lax.axis_size("z")
    own, length_y = flight_fields.shape[3:]
    rows = 2 * own
    length_x = rows * chips
    half = length_y // 2
    block = half // chips
    cells = own * length_y
    tables_x = cas_tables(length_x)
    even_y, even_y_t, odd_y, odd_y_t = tables_x if length_x == length_y else cas_tables(length_y)

    def of(shape, dtype=BF16):
        return jax.ShapeDtypeStruct(shape, dtype)

    def other_core(value):
        return lax.ppermute(value, "core", [(0, 1), (1, 0)])

    fields = flight_fields.reshape(2 * rows, length_y)
    top = top_fields.reshape(2 * rows, length_y)
    mine = slowness[0]
    fields_other, top_other, other = other_core(fields), other_core(top), other_core(mine)
    def factors(stage, odd, behind):
        return call(
            functools.partial(factors_kernel, odd, length_y, stage), (settings,),
            [of((length_x, block), F32)] * 2, flops=400 * cells, name="factors", scalars=1,
            behind=behind,
        )

    def phases(stage, behind):
        return call(
            functools.partial(phase_kernel, stage), (settings, mine, other),
            [of((rows, length_y), F32)] * 2, flops=800 * cells, name="phases", scalars=1,
            behind=behind,
        )

    pieces_of = [of((rows, 2 * block))] * chips
    lines = (2 * rows, half)
    part = pltpu.VMEM(lines, BF16)
    flops = 2 * 2 * rows * half * half
    x_part = pltpu.VMEM((length_x, 2 * block), BF16)

    def exchange(pieces, down=0):
        got = []
        for k, piece in zip(partners(chips), pieces):
            if down:
                pairs = [
                    (d * chips + z, (d + down) % slabs * chips + (z ^ k))
                    for d in range(slabs)
                    for z in range(chips)
                ]
                got.append(lax.ppermute(piece, ("depth", "z"), pairs))
            else:
                pairs = [(z, z ^ k) for z in range(chips)]
                got.append(lax.ppermute(piece, "z", pairs) if k else piece)
        return got

    def along_x(pieces, factor, behind=()):
        return call(
            functools.partial(along_x_kernel, chips), (*factor, *tables_x, *pieces),
            pieces_of, [x_part, x_part], 2 * flops, "along_x", behind=behind,
        )

    def even_part(pieces):
        return call(
            even_part_kernel, (even_y, *pieces), [of(lines, F32)], [part], flops, "even_part"
        )[0]

    share = (rows, half)
    own_evens = call(
        own_modes_kernel, (fields, even_y_t), [of(share)], flops=flops // 2, name="own_modes"
    )[0]
    evens = call(
        even_to_modes_kernel, (fields_other, own_evens, even_y_t),
        pieces_of, [pltpu.VMEM(share, BF16)], flops // 2, "even_to_modes",
    )
    *odds, settings = call(
        odd_to_modes_kernel,
        (flight_blocks, top_block, ref_slowness, fields, fields_other, odd_y_t),
        pieces_of + [of((4,), F32)], [part, part], flops, "odd_to_modes",
        scalars=3, behind=(top_other, other), puts=[VMEM] * chips + [SMEM],
    )
    even_factors, odd_factors = factors(0, 0, ()), factors(0, 1, ())
    first_phases = phases(0, ())
    evens, odds = exchange(evens), exchange(odds)
    evens = exchange(along_x(evens, even_factors, (odd_factors[0], first_phases[0])))
    odds = exchange(along_x(odds, odd_factors))
    *evens, folded, first = call(
        functools.partial(turn_around_kernel, chips),
        (*first_phases, top, top_other, even_y_t, odd_y, even_part(evens), *odds),
        pieces_of + [of(lines), of((2 * rows, length_y))], [part, part], 2 * flops, "turn_around",
    )
    odds = call(odd_modes_kernel, (folded, odd_y_t), pieces_of, [part], flops, "odd_modes")
    ready = (odds[-1],)
    even_factors, odd_factors = factors(1, 0, ready), factors(1, 1, ready)
    second_phases = phases(1, ready)
    evens, odds = exchange(evens, 1), exchange(odds, 1)
    evens = exchange(along_x(evens, even_factors, (odd_factors[0], second_phases[0])))
    odds = along_x(odds, odd_factors)
    first_other = other_core(
        call(other_rows_kernel, (first,), [of((rows, length_y))], name="other_rows", behind=odds[-1:])[0]
    )
    odds = exchange(odds)
    first_part = even_part(evens)
    give, keep = [
        call(
            functools.partial(half_space_kernel, index),
            (*second_phases, odd_y, first_part, *odds),
            [of((rows, length_y))], [pltpu.VMEM((rows, half), BF16)], flops // 2, "half_space",
        )[0]
        for index in (1, 0)
    ]
    got = other_core(give)
    fields, image = call(
        finish_kernel, (first, first_other, keep, got),
        [of((2 * rows, length_y)), of((own, length_y), F32)],
        [pltpu.VMEM((own, length_y), F32), pltpu.SemaphoreType.DMA((4,))],
        flops=8 * cells, name="finish", puts=[HBM] * 2,
    )
    return image[None], fields.reshape(flight_fields.shape)


def passed_along(value, axis, steps):
    count = lax.axis_size(axis)
    leading, last = (max(0, -steps), min(count, count - steps))
    return lax.ppermute(value, axis, [(source, source + steps) for source in range(leading, last)])


def make_table(length):
    positions = jnp.arange(length, dtype=jnp.int32)
    product = positions[:, None] * positions[None, :] % length
    angles = product.astype(jnp.float32) * (2.0 * math.pi / length)
    scaling = 1.0 / math.sqrt(length)
    return (jnp.concatenate([jnp.cos(angles), jnp.sin(angles)], axis=1) * scaling).astype(
        jnp.bfloat16
    )


def wavenumber(positions, length):
    signed = jnp.where(positions < length // 2, positions, positions - length)
    return signed.astype(jnp.float32) * (2.0 * math.pi / length)


def mix(product, along, half_size, orient):
    cosine_part = lax.slice_in_dim(product, 0, half_size, axis=along)
    sine_part = lax.slice_in_dim(product, half_size, 2 * half_size, axis=along)
    real_part = cosine_part[:, 0] + orient * sine_part[:, 1]
    imag_part = cosine_part[:, 1] - orient * sine_part[:, 0]
    return jnp.stack([real_part, imag_part], axis=1)


def rotate(values, cosines, sine_vals):
    real_part = values[:, 0] * cosines - values[:, 1] * sine_vals
    imag_part = values[:, 0] * sine_vals + values[:, 1] * cosines
    return jnp.stack([real_part, imag_part], axis=1)


def spectral(angular, reference_s, wave_x, wave_y):
    quad = (angular * reference_s) ** 2 - wave_x * wave_x - wave_y * wave_y
    travel = jnp.sqrt(jnp.maximum(quad, 0.0)) * step_length
    damping = jnp.exp(-jnp.sqrt(jnp.maximum(-quad, 0.0)) * step_length)
    cosines = damping * jnp.cos(travel)
    sine_vals = damping * jnp.sin(travel)
    return (jnp.stack([cosines, cosines]), jnp.stack([sine_vals, -sine_vals]))


def propagate(fields, spec_cos, spec_sin, space_cos, space_sin, to_cols, to_rows, table_x, table_y):
    length_y = table_y.shape[0]
    length_x = table_x.shape[0]
    product = jnp.einsum("fcry,yk->fckr", fields, table_y, preferred_element_type=jnp.float32)
    first = mix(product, 2, length_y, 1.0).astype(jnp.bfloat16)
    columns = to_cols(first)
    product = jnp.dot(columns, table_x, preferred_element_type=jnp.float32)
    spectrum = mix(product, 3, length_x, 1.0)
    shifted = rotate(spectrum, spec_cos, spec_sin).astype(jnp.bfloat16)
    product = jnp.dot(shifted, table_x, preferred_element_type=jnp.float32)
    back_x = mix(product, 3, length_x, -1.0).astype(jnp.bfloat16)
    rows_back = to_rows(back_x)
    product = jnp.einsum("fckr,ky->fcry", rows_back, table_y, preferred_element_type=jnp.float32)
    space = mix(product, 3, length_y, -1.0)
    return rotate(space, space_cos, space_sin).astype(jnp.bfloat16)


def together_cols(values):
    return lax.all_to_all(values, "trans", split_axis=2, concat_axis=3, tiled=True)


def together_rows(values):
    return lax.all_to_all(values, "trans", split_axis=3, concat_axis=2, tiled=True)


def advance(fields, block_id, slowness, ref_slowness, table_x, table_y):
    length_x = table_x.shape[0]
    length_y = table_y.shape[0]
    trans_count = lax.axis_size("trans")
    local_ky = length_y // trans_count
    ky_rows = lax.axis_index("trans") * local_ky + jnp.arange(local_ky, dtype=jnp.int32)
    wave_y = wavenumber(ky_rows, length_y)[:, None]
    wave_x = wavenumber(jnp.arange(length_x, dtype=jnp.int32), length_x)[None, :]
    angular = omega_top * (block_id.astype(jnp.float32) + 1.0) / NFREQ
    reference_s = ref_slowness[0]
    spec_cos, spec_sin = spectral(angular, reference_s, wave_x, wave_y)
    rotation = angular * (slowness[0] - reference_s) * step_length
    cos_r = jnp.cos(rotation)
    sin_r = jnp.sin(rotation)
    space_cos = jnp.stack([cos_r, cos_r])
    space_sin = jnp.stack([sin_r, -sin_r])
    fields = propagate(
        fields,
        spec_cos,
        spec_sin,
        space_cos,
        space_sin,
        together_cols,
        together_rows,
        table_x,
        table_y,
    )
    values = fields.astype(jnp.float32)
    terms = [values[0, 0] * values[1, 0] + values[0, 1] * values[1, 1]]
    return (fields, jnp.stack(terms))


def general_per_device(flight_fields, top_fields, slowness, ref_slowness, flight_blocks, top_block):
    table_x = make_table(flight_fields.shape[3] * lax.axis_size("trans"))
    table_y = make_table(flight_fields.shape[4])
    depth_idx = lax.axis_index("depth")
    first_block = flight_blocks[depth_idx]
    above_block = flight_blocks[jnp.maximum(depth_idx - 1, 0)]
    second_block = jnp.where(depth_idx == 0, top_block[0], above_block)
    after_first, first_terms = advance(
        flight_fields[0], first_block, slowness, ref_slowness, table_x, table_y
    )
    handed = passed_along(after_first, "depth", 1)
    incoming = jnp.where(depth_idx == 0, top_fields, handed)
    after_second, second_terms = advance(
        incoming, second_block, slowness, ref_slowness, table_x, table_y
    )
    return (first_terms + second_terms, after_second[None])


def solution(mesh):
    slabs, count = mesh.shape["depth"], mesh.shape["trans"]
    chips = count // 2

    def mapped(body, over, trans):
        placed = (
            P("depth", None, None, trans, None),
            P(None, None, trans, None),
            P("depth", trans, None),
            P("depth"),
            P(),
            P(),
        )
        return jax.shard_map(
            body,
            mesh=over,
            in_specs=placed,
            out_specs=(P("depth", trans, None), P("depth", None, None, trans, None)),
            check_vma=False,
        )

    def run(*arrays):
        length_x, length_y = arrays[0].shape[3:]
        fits = count % 2 == 0 and chips & (chips - 1) == 0
        fits = fits and length_y % (256 * chips) == 0 and length_y % 512 == 0
        if not fits or length_x % (32 * chips) or length_x % 128:
            return mapped(general_per_device, mesh, "trans")(*arrays)
        cores = Mesh(mesh.devices.reshape(slabs, chips, 2), ("depth", "z", "core"))
        return mapped(per_device, cores, ("z", "core"))(*arrays)

    return run
```

```python
import functools
import math

import jax
import jax.numpy as jnp
import numpy as np
from jax import lax
from jax.experimental import pallas as pl
from jax.experimental.pallas import tpu as pltpu
from jax.sharding import Mesh, PartitionSpec as P

NFREQ = 256

omega_top = 4.0
step_length = 0.5

VMEM = pl.BlockSpec(memory_space=pltpu.VMEM)
SMEM = pl.BlockSpec(memory_space=pltpu.SMEM)
ANY = pl.BlockSpec(memory_space=pl.ANY)
HBM = pl.BlockSpec(memory_space=pltpu.HBM)
F32 = jnp.float32
BF16 = jnp.bfloat16


def partners(count):
    return sorted(range(count), key=lambda k: (-k.bit_length(), k))


def cas_tables(length):
    positions = np.arange(length // 2, dtype=np.int64)
    quarter = length // 4

    def table(low):
        modes = np.concatenate([low, np.where(low == 0, length // 2, -low)])
        angles = (modes[:, None] * positions[None, :] % length) * (2.0 * math.pi / length)
        return ((np.cos(angles) + np.sin(angles)) / math.sqrt(length)).astype(jnp.bfloat16)

    both = [table(2 * positions[:quarter] + odd) for odd in (0, 1)]
    return [jnp.asarray(t) for one in both for t in (one, one.T.copy())]


def wave(index, length, odd):
    quarter = length // 4
    low = jnp.where(index < quarter, index, index - quarter)
    mode = 2 * low + odd
    if not odd:
        mode = jnp.where(index == quarter, length // 2, mode)
    return mode.astype(F32) * (2.0 * math.pi / length)


def dot(left, right):
    return jnp.dot(left, right, preferred_element_type=F32)


def fitted(function, degree):
    nodes = 2.1 * (1.0 + np.cos(math.pi * (np.arange(64) + 0.5) / 64))
    fit = np.polynomial.Chebyshev.fit(nodes, function(np.sqrt(nodes)), degree, domain=[0, 4.2])
    return [float(c) for c in fit.convert(kind=np.polynomial.Polynomial).coef]


COSINE = fitted(np.cos, 5)
SINE = fitted(lambda angle: np.sin(angle) / angle, 5)


def field_sign():
    return jnp.where(lax.axis_index("core") == 1, -1.0, 1.0)


def cos_sin(angle):
    square = angle * angle
    cosine = jnp.full_like(square, COSINE[-1])
    for coefficient in COSINE[-2::-1]:
        cosine = cosine * square + coefficient
    sine = jnp.full_like(square, SINE[-1])
    for coefficient in SINE[-2::-1]:
        sine = sine * square + coefficient
    return cosine, sine * angle


def factors_kernel(odd, length_y, stage, settings_ref, cos_ref, sin_ref):
    length_x, modes = cos_ref.shape
    quarter = length_x // 4
    angular, reference_s = settings_ref[2 * stage], settings_ref[2 * stage + 1]
    sign = field_sign()
    step = min(64, quarter)
    lane = lax.broadcasted_iota(jnp.int32, (step, modes), 1)
    line = lax.broadcasted_iota(jnp.int32, (step, modes), 0)
    wave_y = wave(lax.axis_index("z") * modes + lane, length_y, odd)
    constant = (angular * reference_s) ** 2 - wave_y * wave_y

    def work_out(wave_x, constant):
        quad = constant - wave_x * wave_x
        root = jnp.sqrt(jnp.abs(quad)) * step_length
        travels = quad > 0.0
        cosine, sine = cos_sin(jnp.where(travels, root, 0.0))
        damping = jnp.exp(jnp.where(travels, 0.0, -root))
        return damping * cosine, (sign * damping) * sine

    for x_odd in range(2):
        for start in range(0, quarter, step):
            values = work_out(wave(start + line, length_x, x_odd), constant)
            for half in range(2):
                at = (2 * x_odd + half) * quarter + start
                cos_ref[at : at + step, :], sin_ref[at : at + step, :] = values
    values = work_out(wave(quarter + line[:8], length_x, 0), constant[:8])
    cos_ref[quarter : quarter + 8, :], sin_ref[quarter : quarter + 8, :] = values


def phase_kernel(stage, settings_ref, mine_ref, other_ref, cos_ref, sin_ref):
    angular, reference_s = settings_ref[2 * stage], settings_ref[2 * stage + 1]
    sign = field_sign()
    rows = mine_ref.shape[0]
    step = 8
    for index, slowness in enumerate((mine_ref, other_ref)):
        start = (lax.axis_index("core") ^ index) * rows

        @pl.loop(0, rows // step)
        def _(chunk):
            there = pl.ds(pl.multiple_of(start + chunk * step, step), step)
            here = pl.ds(pl.multiple_of(chunk * step, step), step)
            cosine, sine = cos_sin(angular * (slowness[here, :] - reference_s) * step_length)
            cos_ref[there, :] = cosine
            sin_ref[there, :] = sign * sine


def rows_of(start, size):
    return pl.ds(pl.multiple_of(start, size), size)


def split_modes(here, whole, outs):
    rows, width = outs[0].shape
    block = width // 2
    for k, out in zip(partners(len(outs)), outs):
        columns = rows_of((here ^ k) * block, block)
        for part in range(2):
            out[:, part * block : (part + 1) * block] = whole[
                part * rows : (part + 1) * rows, columns
            ]


def join_modes(here, pieces, whole, lines=None):
    rows, width = pieces[0].shape
    block = width // 2
    size = rows if lines is None else lines.size
    for k, piece in zip(partners(len(pieces)), pieces):
        columns = rows_of((here ^ k) * block, block)
        for part in range(2):
            whole[part * size : (part + 1) * size, columns] = piece[
                slice(None) if lines is None else lines, part * block : (part + 1) * block
            ]


def all_pieces(sign, fields_ref, other_ref, table_ref, *refs):
    outs, (folded, modes) = refs[:-2], refs[-2:]
    half = table_ref.shape[0]
    own = folded.shape[0] // 4
    core = lax.axis_index("core")
    for part in range(2):
        mine = rows_of((2 * core + part) * own, own)
        for index, source in enumerate((fields_ref, other_ref)):
            there = rows_of(2 * part * own + (core ^ index) * own, own)
            folded[there, :] = source[mine, :half] + sign * source[mine, half:]
    modes[...] = dot(folded[...], table_ref[...]).astype(BF16)
    split_modes(lax.axis_index("z"), modes, outs)


def odd_to_modes_kernel(blocks_ref, top_block_ref, reference_ref, *refs):
    settings_ref = refs[-3]
    depth = lax.axis_index("depth")
    above = blocks_ref[jnp.maximum(depth - 1, 0)]
    second = jnp.where(depth == 0, top_block_ref[0], above)
    for index, block in enumerate((blocks_ref[depth], second)):
        settings_ref[2 * index] = omega_top * (block.astype(F32) + 1.0) / NFREQ
        settings_ref[2 * index + 1] = reference_ref[0]
    all_pieces(-1, *refs[:-3], *refs[-2:])


def along_x_kernel(
    count, cos_ref, sin_ref, even_ref, even_t_ref, odd_ref, odd_t_ref, *refs
):
    pieces, outs = refs[:count], refs[count : 2 * count]
    held, shifted = refs[2 * count :]
    here = lax.axis_index("z")
    rows, width = outs[0].shape
    block = width // 2
    for k, piece in zip(partners(count), pieces):
        held[rows_of((here ^ k) * rows, rows), :] = piece[...]
    half = even_ref.shape[0]
    low, high = held[:half, :], held[half:, :]
    for part, table, values in ((0, even_ref, low + high), (1, odd_ref, low - high)):
        lines = slice(part * half, (part + 1) * half)
        spectrum = dot(table[...], values)
        real, imag = spectrum[:, :block], spectrum[:, block:]
        cosine, sine = cos_ref[lines, :], sin_ref[lines, :]
        shifted[lines, :block] = (real * cosine - imag * sine).astype(BF16)
        shifted[lines, block:] = (real * sine + imag * cosine).astype(BF16)
    first = dot(even_t_ref[...], shifted[:half, :])
    second = dot(odd_t_ref[...], shifted[half:, :])
    held[:half, :] = (first + second).astype(BF16)
    held[half:, :] = (first - second).astype(BF16)
    for k, out in zip(partners(count), outs):
        out[...] = held[rows_of((here ^ k) * rows, rows), :]


def even_part_kernel(table_ref, *refs):
    pieces, (out_ref, modes) = refs[:-2], refs[-2:]
    join_modes(lax.axis_index("z"), pieces, modes)
    out_ref[...] = dot(modes[...], table_ref[...])


def turned(real, imag, cosine, sine):
    return (real * cosine - imag * sine).astype(BF16), (real * sine + imag * cosine).astype(BF16)


def turn_around_kernel(
    count, cos_ref, sin_ref, top_ref, top_other_ref, even_t_ref, odd_ref, part_ref, *refs
):
    pieces, outs = refs[:count], refs[count : 2 * count]
    folded_ref, both_ref, modes, sums = refs[2 * count :]
    here, core = lax.axis_index("z"), lax.axis_index("core")
    rows = pieces[0].shape[0]
    own = rows // 2
    half = odd_ref.shape[0]
    join_modes(here, pieces, modes)
    step = 512
    for start in range(0, half, step):
        columns = slice(start, start + step)
        second = dot(modes[...], odd_ref[:, columns])
        first = part_ref[:, columns]
        stepped = []
        for values, at in ((first + second, start), (first - second, start + half)):
            lanes = slice(at, at + step)
            fields = turned(values[:rows], values[rows:], cos_ref[:, lanes], sin_ref[:, lanes])
            stepped.append(fields)
            for index in range(2):
                for part, field in enumerate(fields):
                    there = (2 * index + part) * own
                    both_ref[there : there + own, lanes] = field[index * own : (index + 1) * own]
        for part in range(2):
            lines = slice(part * rows, (part + 1) * rows)
            sums[lines, columns] = stepped[0][part] + stepped[1][part]
            folded_ref[lines, columns] = stepped[0][part] - stepped[1][part]

    @pl.when(lax.axis_index("depth") == lax.axis_size("depth") - 1)
    def _():
        for index, source in enumerate((top_ref, top_other_ref)):
            for part in range(2):
                lines = rows_of((2 * core + part) * own, own)
                low, high = source[lines, :half], source[lines, half:]
                there = rows_of(part * rows + (core ^ index) * own, own)
                sums[there, :] = low + high
                folded_ref[there, :] = low - high

    modes[...] = dot(sums[...], even_t_ref[...]).astype(BF16)
    split_modes(here, modes, outs)


def odd_modes_kernel(folded_ref, table_ref, *refs):
    outs, modes = refs[:-1], refs[-1]
    modes[...] = dot(folded_ref[...], table_ref[...]).astype(BF16)
    split_modes(lax.axis_index("z"), modes, outs)


def half_space_kernel(index, cos_ref, sin_ref, odd_ref, part_ref, *refs):
    pieces, (out_ref, modes) = refs[:-2], refs[-2:]
    rows = pieces[0].shape[0]
    own = rows // 2
    half = odd_ref.shape[0]
    offset = (lax.axis_index("core") ^ index) * own
    lines = rows_of(offset, own)
    join_modes(lax.axis_index("z"), pieces, modes, lines)
    step = 512
    for start in range(0, half, step):
        columns = slice(start, start + step)
        second = dot(modes[...], odd_ref[:, columns])
        for sign, at in ((1.0, start), (-1.0, start + half)):
            lanes = slice(at, at + step)
            real, imag = [
                part_ref[rows_of(part * rows + offset, own), columns]
                + sign * second[part * own : (part + 1) * own]
                for part in range(2)
            ]
            out_ref[:own, lanes], out_ref[own:, lanes] = turned(
                real, imag, cos_ref[lines, lanes], sin_ref[lines, lanes]
            )


def other_rows_kernel(both_ref, out_ref):
    rows = out_ref.shape[0]
    out_ref[...] = both_ref[rows_of((lax.axis_index("core") ^ 1) * rows, rows), :]


def finish_kernel(
    first_ref, first_other_ref, keep_ref, got_ref, fields_out, image_out, image, sems
):
    rows = keep_ref.shape[0]
    own = rows // 2
    core = lax.axis_index("core")
    copies = [
        pltpu.make_async_copy(keep_ref, fields_out.at[rows_of(core * rows, rows), :], sems.at[0]),
        pltpu.make_async_copy(
            got_ref, fields_out.at[rows_of((core ^ 1) * rows, rows), :], sems.at[1]
        ),
    ]
    for copy in copies:
        copy.start()
    step = 16
    for start in range(0, own, step):
        total = None
        for part in range(2):
            lines = slice(part * own + start, part * own + start + step)
            mine = rows_of(core * rows + part * own + start, step)
            for one, two in (
                (first_ref[mine, :], first_other_ref[lines, :]),
                (keep_ref[lines, :], got_ref[lines, :]),
            ):
                term = one.astype(F32) * two.astype(F32)
                total = term if total is None else total + term
        image[start : start + step, :] = total
        if (start + step) % (own // 2) == 0:
            done = slice(start + step - own // 2, start + step)
            copies.append(
                pltpu.make_async_copy(
                    image.at[done, :], image_out.at[done, :], sems.at[len(copies)]
                )
            )
            copies[-1].start()
    for copy in copies:
        copy.wait()


def after(count, kernel, *refs):
    return kernel(*refs[count:])


def call(
    kernel, operands, outs, scratch=(), flops=0, name=None, scalars=0, behind=(), ins=None, puts=None,
    grant=24,
):
    moved = sum(math.prod(a.shape) * a.dtype.itemsize for a in operands)
    moved += sum(math.prod(a.shape) * a.dtype.itemsize for a in outs)
    return pl.pallas_call(
        functools.partial(after, len(behind), kernel),
        out_shape=tuple(outs),
        in_specs=[ANY] * len(behind)
        + (ins or [SMEM] * scalars + [VMEM] * (len(operands) - scalars)),
        out_specs=tuple(puts or [VMEM] * len(outs)),
        scratch_shapes=list(scratch),
        compiler_params=pltpu.CompilerParams(vmem_limit_bytes=grant * 1024 * 1024),
        cost_estimate=pl.CostEstimate(flops=flops, bytes_accessed=moved, transcendentals=0),
        name=name,
    )(*behind, *operands)


def per_device(flight_fields, top_fields, slowness, ref_slowness, flight_blocks, top_block):
    slabs, chips = lax.axis_size("depth"), lax.axis_size("z")
    own, length_y = flight_fields.shape[3:]
    rows = 2 * own
    length_x = rows * chips
    half = length_y // 2
    block = half // chips
    cells = own * length_y
    tables_x = cas_tables(length_x)
    even_y, even_y_t, odd_y, odd_y_t = tables_x if length_x == length_y else cas_tables(length_y)

    def of(shape, dtype=BF16):
        return jax.ShapeDtypeStruct(shape, dtype)

    def other_core(value):
        return lax.ppermute(value, "core", [(0, 1), (1, 0)])

    fields = flight_fields.reshape(2 * rows, length_y)
    top = top_fields.reshape(2 * rows, length_y)
    mine = slowness[0]
    fields_other, top_other, other = other_core(fields), other_core(top), other_core(mine)
    def factors(stage, odd, behind):
        return call(
            functools.partial(factors_kernel, odd, length_y, stage), (settings,),
            [of((length_x, block), F32)] * 2, flops=400 * cells, name="factors", scalars=1,
            behind=behind,
        )

    def phases(stage, behind):
        return call(
            functools.partial(phase_kernel, stage), (settings, mine, other),
            [of((rows, length_y), F32)] * 2, flops=800 * cells, name="phases", scalars=1,
            behind=behind,
        )

    pieces_of = [of((rows, 2 * block))] * chips
    lines = (2 * rows, half)
    part = pltpu.VMEM(lines, BF16)
    flops = 2 * 2 * rows * half * half
    x_part = pltpu.VMEM((length_x, 2 * block), BF16)

    def exchange(pieces, down=0):
        got = []
        for k, piece in zip(partners(chips), pieces):
            if down:
                pairs = [
                    (d * chips + z, (d + down) % slabs * chips + (z ^ k))
                    for d in range(slabs)
                    for z in range(chips)
                ]
                got.append(lax.ppermute(piece, ("depth", "z"), pairs))
            else:
                pairs = [(z, z ^ k) for z in range(chips)]
                got.append(lax.ppermute(piece, "z", pairs) if k else piece)
        return got

    def along_x(pieces, factor, behind=()):
        return call(
            functools.partial(along_x_kernel, chips), (*factor, *tables_x, *pieces),
            pieces_of, [x_part, x_part], 2 * flops, "along_x", behind=behind,
        )

    def even_part(pieces):
        return call(
            even_part_kernel, (even_y, *pieces), [of(lines, F32)], [part], flops, "even_part"
        )[0]

    share = (rows, half)
    evens = call(
        functools.partial(all_pieces, 1), (fields, fields_other, even_y_t),
        pieces_of, [part, part], flops, "even_to_modes",
    )
    *odds, settings = call(
        odd_to_modes_kernel,
        (flight_blocks, top_block, ref_slowness, fields, fields_other, odd_y_t),
        pieces_of + [of((4,), F32)], [part, part], flops, "odd_to_modes",
        scalars=3, behind=(top_other, other), puts=[VMEM] * chips + [SMEM],
    )
    even_factors, odd_factors = factors(0, 0, ()), factors(0, 1, ())
    first_phases = phases(0, ())
    evens, odds = exchange(evens), exchange(odds)
    evens = exchange(along_x(evens, even_factors, (odd_factors[0], first_phases[0])))
    odds = exchange(along_x(odds, odd_factors))
    *evens, folded, first = call(
        functools.partial(turn_around_kernel, chips),
        (*first_phases, top, top_other, even_y_t, odd_y, even_part(evens), *odds),
        pieces_of + [of(lines), of((2 * rows, length_y))], [part, part], 2 * flops, "turn_around",
    )
    odds = call(odd_modes_kernel, (folded, odd_y_t), pieces_of, [part], flops, "odd_modes")
    ready = (odds[-1],)
    even_factors, odd_factors = factors(1, 0, ready), factors(1, 1, ready)
    second_phases = phases(1, ready)
    evens, odds = exchange(evens, 1), exchange(odds, 1)
    evens = exchange(along_x(evens, even_factors, (odd_factors[0], second_phases[0])))
    odds = along_x(odds, odd_factors)
    first_other = other_core(
        call(other_rows_kernel, (first,), [of((rows, length_y))], name="other_rows", behind=odds[-1:])[0]
    )
    odds = exchange(odds)
    first_part = even_part(evens)
    give, keep = [
        call(
            functools.partial(half_space_kernel, index),
            (*second_phases, odd_y, first_part, *odds),
            [of((rows, length_y))], [pltpu.VMEM((rows, half), BF16)], flops // 2, "half_space",
        )[0]
        for index in (1, 0)
    ]
    got = other_core(give)
    fields, image = call(
        finish_kernel, (first, first_other, keep, got),
        [of((2 * rows, length_y)), of((own, length_y), F32)],
        [pltpu.VMEM((own, length_y), F32), pltpu.SemaphoreType.DMA((4,))],
        flops=8 * cells, name="finish", puts=[HBM] * 2,
    )
    return image[None], fields.reshape(flight_fields.shape)


def passed_along(value, axis, steps):
    count = lax.axis_size(axis)
    leading, last = (max(0, -steps), min(count, count - steps))
    return lax.ppermute(value, axis, [(source, source + steps) for source in range(leading, last)])


def make_table(length):
    positions = jnp.arange(length, dtype=jnp.int32)
    product = positions[:, None] * positions[None, :] % length
    angles = product.astype(jnp.float32) * (2.0 * math.pi / length)
    scaling = 1.0 / math.sqrt(length)
    return (jnp.concatenate([jnp.cos(angles), jnp.sin(angles)], axis=1) * scaling).astype(
        jnp.bfloat16
    )


def wavenumber(positions, length):
    signed = jnp.where(positions < length // 2, positions, positions - length)
    return signed.astype(jnp.float32) * (2.0 * math.pi / length)


def mix(product, along, half_size, orient):
    cosine_part = lax.slice_in_dim(product, 0, half_size, axis=along)
    sine_part = lax.slice_in_dim(product, half_size, 2 * half_size, axis=along)
    real_part = cosine_part[:, 0] + orient * sine_part[:, 1]
    imag_part = cosine_part[:, 1] - orient * sine_part[:, 0]
    return jnp.stack([real_part, imag_part], axis=1)


def rotate(values, cosines, sine_vals):
    real_part = values[:, 0] * cosines - values[:, 1] * sine_vals
    imag_part = values[:, 0] * sine_vals + values[:, 1] * cosines
    return jnp.stack([real_part, imag_part], axis=1)


def spectral(angular, reference_s, wave_x, wave_y):
    quad = (angular * reference_s) ** 2 - wave_x * wave_x - wave_y * wave_y
    travel = jnp.sqrt(jnp.maximum(quad, 0.0)) * step_length
    damping = jnp.exp(-jnp.sqrt(jnp.maximum(-quad, 0.0)) * step_length)
    cosines = damping * jnp.cos(travel)
    sine_vals = damping * jnp.sin(travel)
    return (jnp.stack([cosines, cosines]), jnp.stack([sine_vals, -sine_vals]))


def propagate(fields, spec_cos, spec_sin, space_cos, space_sin, to_cols, to_rows, table_x, table_y):
    length_y = table_y.shape[0]
    length_x = table_x.shape[0]
    product = jnp.einsum("fcry,yk->fckr", fields, table_y, preferred_element_type=jnp.float32)
    first = mix(product, 2, length_y, 1.0).astype(jnp.bfloat16)
    columns = to_cols(first)
    product = jnp.dot(columns, table_x, preferred_element_type=jnp.float32)
    spectrum = mix(product, 3, length_x, 1.0)
    shifted = rotate(spectrum, spec_cos, spec_sin).astype(jnp.bfloat16)
    product = jnp.dot(shifted, table_x, preferred_element_type=jnp.float32)
    back_x = mix(product, 3, length_x, -1.0).astype(jnp.bfloat16)
    rows_back = to_rows(back_x)
    product = jnp.einsum("fckr,ky->fcry", rows_back, table_y, preferred_element_type=jnp.float32)
    space = mix(product, 3, length_y, -1.0)
    return rotate(space, space_cos, space_sin).astype(jnp.bfloat16)


def together_cols(values):
    return lax.all_to_all(values, "trans", split_axis=2, concat_axis=3, tiled=True)


def together_rows(values):
    return lax.all_to_all(values, "trans", split_axis=3, concat_axis=2, tiled=True)


def advance(fields, block_id, slowness, ref_slowness, table_x, table_y):
    length_x = table_x.shape[0]
    length_y = table_y.shape[0]
    trans_count = lax.axis_size("trans")
    local_ky = length_y // trans_count
    ky_rows = lax.axis_index("trans") * local_ky + jnp.arange(local_ky, dtype=jnp.int32)
    wave_y = wavenumber(ky_rows, length_y)[:, None]
    wave_x = wavenumber(jnp.arange(length_x, dtype=jnp.int32), length_x)[None, :]
    angular = omega_top * (block_id.astype(jnp.float32) + 1.0) / NFREQ
    reference_s = ref_slowness[0]
    spec_cos, spec_sin = spectral(angular, reference_s, wave_x, wave_y)
    rotation = angular * (slowness[0] - reference_s) * step_length
    cos_r = jnp.cos(rotation)
    sin_r = jnp.sin(rotation)
    space_cos = jnp.stack([cos_r, cos_r])
    space_sin = jnp.stack([sin_r, -sin_r])
    fields = propagate(
        fields,
        spec_cos,
        spec_sin,
        space_cos,
        space_sin,
        together_cols,
        together_rows,
        table_x,
        table_y,
    )
    values = fields.astype(jnp.float32)
    terms = [values[0, 0] * values[1, 0] + values[0, 1] * values[1, 1]]
    return (fields, jnp.stack(terms))


def general_per_device(flight_fields, top_fields, slowness, ref_slowness, flight_blocks, top_block):
    table_x = make_table(flight_fields.shape[3] * lax.axis_size("trans"))
    table_y = make_table(flight_fields.shape[4])
    depth_idx = lax.axis_index("depth")
    first_block = flight_blocks[depth_idx]
    above_block = flight_blocks[jnp.maximum(depth_idx - 1, 0)]
    second_block = jnp.where(depth_idx == 0, top_block[0], above_block)
    after_first, first_terms = advance(
        flight_fields[0], first_block, slowness, ref_slowness, table_x, table_y
    )
    handed = passed_along(after_first, "depth", 1)
    incoming = jnp.where(depth_idx == 0, top_fields, handed)
    after_second, second_terms = advance(
        incoming, second_block, slowness, ref_slowness, table_x, table_y
    )
    return (first_terms + second_terms, after_second[None])


def solution(mesh):
    slabs, count = mesh.shape["depth"], mesh.shape["trans"]
    chips = count // 2

    def mapped(body, over, trans):
        placed = (
            P("depth", None, None, trans, None),
            P(None, None, trans, None),
            P("depth", trans, None),
            P("depth"),
            P(),
            P(),
        )
        return jax.shard_map(
            body,
            mesh=over,
            in_specs=placed,
            out_specs=(P("depth", trans, None), P("depth", None, None, trans, None)),
            check_vma=False,
        )

    def run(*arrays):
        length_x, length_y = arrays[0].shape[3:]
        fits = count % 2 == 0 and chips & (chips - 1) == 0
        fits = fits and length_y % (256 * chips) == 0 and length_y % 512 == 0
        if not fits or length_x % (32 * chips) or length_x % 128:
            return mapped(general_per_device, mesh, "trans")(*arrays)
        cores = Mesh(mesh.devices.reshape(slabs, chips, 2), ("depth", "z", "core"))
        return mapped(per_device, cores, ("z", "core"))(*arrays)

    return run
```
